32 devices in a mesh: groups: 2 (over x), slab: 16 (over z, y, core).
Axes of the slice: x: 2, y: 2, z: 4, core: 2. Of those that a mesh axis runs over, the one named last changes fastest.
Arguments:
- trial_modes: bfloat16 [32, 4096, 384], P(('groups', 'slab')), parts along dimension 0, may hold values from -6 to 6
- onsite_blocks: bfloat16 [32, 96, 128, 128], P(('groups', 'slab')), parts along dimension 0, may hold values from -18 to 18
- onsite_rows: int32 [32, 96], P(('groups', 'slab')), parts along dimension 0, may hold values from 0 to 31
- onsite_cols: int32 [32, 96], P(('groups', 'slab')), parts along dimension 0, may hold values from 0 to 31
- coupling_blocks: bfloat16 [32, 16, 128, 128], P(('groups', 'slab')), parts along dimension 0, may hold values from -48 to 48
- coupling_rows: int32 [32, 16], P(('groups', 'slab')), parts along dimension 0, may hold values from 28 to 31
- coupling_cols: int32 [32, 16], P(('groups', 'slab')), parts along dimension 0, may hold values from 0 to 3
- potential_step: float32 [32], P(('groups', 'slab')), parts along dimension 0, may hold values from -0.6 to 0.6
Outputs:
- onsite_reduced: float32 [32, 384, 384], P(('groups', 'slab')), parts along dimension 0
- coupling_right: float32 [32, 384, 384], P(('groups', 'slab')), parts along dimension 0
- coupling_left: float32 [32, 384, 384], P(('groups', 'slab')), parts along dimension 0
The draws below stay inside these ranges and needn't reach their ends.
There are 2 independent parts, one for each index of `groups`. The reference program is written for one: setup_inputs(seed, part) draws one part's arguments, and reference() takes and returns one part's arrays. A program takes and returns all parts, laid end to end along the dimension named above; each array names one. Nothing has to cross between parts.
Inputs may be any that keep to these rules, and one draw needn't show every extreme that they name: `coupling_cols`: every coupling block lies in the last 4 block rows of its slab and the first 4 block columns of the next slab.
All inputs are finite; a program needn't handle non-finite values.
Results may differ from the reference program's by a relative error of at most 0.0067.
Values may be sent and summed in bfloat16 or wider, within the bound.
No kernel may reach another device: no remote copies, remote signals or barrier semaphores. Data moves between devices by JAX's collectives and lax.ppermute only.
A program may use at most 128 MiB of HBM per device.

```python
import jax
import jax.numpy as jnp
from jax import lax

NORB = 4096
MODES = 384
BLK = 128
NNZ = 96
SURF = 4
NCPL = 16
SLAB_DEV = 1
NB = 32
NSLAB = 16


def draw_potential_step(key, part):
    key = jax.random.fold_in(key, 7)
    positions = jnp.arange(NSLAB, dtype=jnp.int32) // SLAB_DEV
    sign_values = (1 - 2 * (positions % 2)).astype(jnp.float32)
    magnitude = jax.random.uniform(key, (NSLAB,), jnp.float32, 0.25, 0.6)
    return sign_values * magnitude


def plant(drawn, rng, smallest, high):
    longest = drawn.shape.index(max(drawn.shape))
    spots = []
    for shift in (0, 1):
        where = [jax.random.randint(jax.random.fold_in(rng, axis), (), 0, length) for axis, length in enumerate(drawn.shape)]
        where[longest] = (where[longest] + shift) % drawn.shape[longest]
        spots.append(tuple(where))
    return drawn.at[spots[0]].set(smallest).at[spots[1]].set(high)


def levels(stream_key, shape, pieces, low, top_value):
    level = 1.0
    for dim, parts in pieces:
        heights = jax.random.uniform(jax.random.fold_in(jax.random.fold_in(stream_key, 6), dim), (parts,), jnp.float32, low / len(pieces), top_value / len(pieces))
        level = level * jnp.repeat(jnp.exp(heights), shape[dim] // parts).reshape((-1,) + (1,) * (len(shape) - 1 - dim))
    return level


def centred(stream_key, extent, scale, limit, split=(), kind=jnp.bfloat16):
    gain = levels(stream_key, extent, split, -0.22, 0.18) if split else 1.0
    entries = jax.random.normal(stream_key, extent, jnp.float32) * scale * gain
    return jnp.minimum(jnp.maximum(entries, -limit), limit).astype(kind)


def setup_inputs(seed: int = 0, part: int = 0) -> dict:
    key_of = jax.random.split(jax.random.key(seed), 9)
    part_keys = jax.random.split(jax.random.fold_in(key_of[8], part), 9)
    return {
        "trial_modes": centred(part_keys[0], (NSLAB, NORB, MODES), 1.0, 6.0, ((0, 16),)),
        "onsite_blocks": centred(part_keys[1], (NSLAB, NNZ, BLK, BLK), 3.0, 18.0, ((0, 16),)),
        "onsite_rows": plant(jax.random.randint(part_keys[2], (NSLAB, NNZ), 0, NB), jax.random.fold_in(part_keys[2], 1), 0, NB - 1).astype(jnp.int32),
        "onsite_cols": plant(jax.random.randint(part_keys[3], (NSLAB, NNZ), 0, NB), jax.random.fold_in(part_keys[3], 1), 0, NB - 1).astype(jnp.int32),
        "coupling_blocks": centred(part_keys[4], (NSLAB, NCPL, BLK, BLK), 8.0, 48.0, ((0, 16),)),
        "coupling_rows": plant(jax.random.randint(part_keys[5], (NSLAB, NCPL), NB - SURF, NB), jax.random.fold_in(part_keys[5], 1), NB - SURF, NB - 1).astype(jnp.int32),
        "coupling_cols": plant(jax.random.randint(part_keys[6], (NSLAB, NCPL), 0, SURF), jax.random.fold_in(part_keys[6], 1), 0, SURF - 1).astype(jnp.int32),
        "potential_step": draw_potential_step(jax.random.fold_in(jax.random.fold_in(key_of[8], part), 71), part),
    }


def orthonormal(trial_rows):
    gram_matrix = jnp.dot(trial_rows.T.astype(jnp.float32), trial_rows.astype(jnp.float32), preferred_element_type=jnp.float32)
    lower_factor = jnp.linalg.cholesky(gram_matrix)
    inverse = jax.scipy.linalg.solve_triangular(lower_factor, jnp.eye(MODES, dtype=jnp.float32), lower=True)
    factor = inverse.T.astype(jnp.bfloat16)
    return jnp.dot(trial_rows.astype(jnp.float32), factor.astype(jnp.float32), preferred_element_type=jnp.float32).astype(jnp.bfloat16)

def block_product(basis_rows, blocks, block_rows, block_cols):
    tile_rows = basis_rows.reshape(NB, BLK, MODES)
    picked = tile_rows[block_cols.astype(jnp.int32)].astype(jnp.float32)
    products = jnp.einsum('jab,jbm->jam', blocks.astype(jnp.float32), picked, precision=lax.Precision.HIGHEST)
    summed = jax.ops.segment_sum(products, block_rows.astype(jnp.int32), num_segments=NB)
    return summed.astype(jnp.bfloat16).reshape(NORB, MODES)

def reference(trial_modes, onsite_blocks, onsite_rows, onsite_cols, coupling_blocks, coupling_rows, coupling_cols, potential_step):
    basis_all = lax.map(orthonormal, trial_modes)

    def onsite_one(item):
        basis_rows, blocks, block_rows, block_cols = item
        spread = block_product(basis_rows, blocks, block_rows, block_cols)
        return jnp.dot(basis_rows.T.astype(jnp.float32), spread.astype(jnp.float32), preferred_element_type=jnp.float32)
    inner = lax.map(onsite_one, (basis_all, onsite_blocks, onsite_rows, onsite_cols))
    potential = jnp.cumsum(potential_step)
    onsite_reduced = inner + jnp.swapaxes(inner, 1, 2) + potential[:, None, None] * jnp.eye(MODES, dtype=jnp.float32)

    def coupling_one(item):
        here_rows, next_rows, blocks, block_rows, block_cols = item
        hop = block_product(next_rows, blocks, block_rows, block_cols)
        return jnp.dot(here_rows.T.astype(jnp.float32), hop.astype(jnp.float32), preferred_element_type=jnp.float32)
    couple = lax.map(coupling_one, (basis_all[:-1], basis_all[1:], coupling_blocks[:-1], coupling_rows[:-1], coupling_cols[:-1]))
    zero_block = jnp.zeros((1, MODES, MODES), jnp.float32)
    coupling_right = jnp.concatenate([couple, zero_block], axis=0)
    coupling_left = jnp.concatenate([zero_block, jnp.swapaxes(couple, 1, 2)], axis=0)
    return (onsite_reduced, coupling_right, coupling_left)
```

```python
import functools

import jax
import jax.numpy as jnp
from jax import lax
from jax.experimental import pallas as pl
from jax.experimental.pallas import tpu as pltpu
from jax.sharding import PartitionSpec as P

F32 = jnp.float32
BF16 = jnp.bfloat16
VMEM_LIMIT = 56 * 1024 * 1024
SURFACE = 4
TILE = 128
ROWS = 8


def lane(value, k):
    return jnp.broadcast_to(value[:, k : k + 1], value.shape)


def row(value, k):
    return jnp.broadcast_to(value[k : k + 1, :], value.shape)


def exact_dot(a, b, dims):
    return lax.dot_general(
        a, b, (dims, ((), ())), precision=lax.Precision.HIGHEST, preferred_element_type=F32
    )


def bf_dot(a, b, dims):
    return lax.dot_general(a, b, (dims, ((), ())), preferred_element_type=F32)


NN = ((1,), (0,))
TN = ((0,), (0,))
NT = ((1,), (1,))


def factor_tile(a_rows, x_rows):
    panels = len(a_rows)
    for g in range(panels):
        here, here_x = a_rows[g], x_rows[g]
        columns = [lane(here, ROWS * g + j) for j in range(ROWS)]
        s = {(i, j): row(columns[j], i) for j in range(ROWS) for i in range(j, ROWS)}
        r = []
        for k in range(ROWS):
            r.append(lax.rsqrt(s[k, k]))
            for i in range(k + 1, ROWS):
                s[i, k] = s[i, k] * r[k]
            for j in range(k + 1, ROWS):
                for i in range(j, ROWS):
                    s[i, j] = s[i, j] - s[i, k] * s[j, k]
        z, zx = [], []
        for k in range(ROWS):
            top, top_x = row(here, k), row(here_x, k)
            for m in range(k):
                top = top - s[k, m] * z[m]
                top_x = top_x - s[k, m] * zx[m]
            z.append(top * r[k])
            zx.append(top_x * r[k])
        sub = lax.broadcasted_iota(jnp.int32, here.shape, 0)
        packed_x = zx[0]
        for k in range(1, ROWS):
            packed_x = jnp.where(sub == k, zx[k], packed_x)
        x_rows[g] = packed_x
        for i in range(g + 1, panels):
            below = []
            for k in range(ROWS):
                c = lane(a_rows[i], ROWS * g + k)
                for m in range(k):
                    c = c - below[m] * s[k, m]
                below.append(c * r[k])
            a_rows[i] = a_rows[i] - sum(below[k] * z[k] for k in range(ROWS))
            x_rows[i] = x_rows[i] - sum(below[k] * zx[k] for k in range(ROWS))
    return x_rows


def factor_kernel(u_hbm, f_ref, head_ref, tail_ref, u_ref, gram_ref, inv_ref, x_ref, sems):
    orbitals, modes = u_ref.shape
    chunks = sems.shape[0]
    step = orbitals // chunks
    copies = [
        pltpu.make_async_copy(
            u_hbm.at[pl.ds(c * step, step)], u_ref.at[pl.ds(c * step, step)], sems.at[c]
        )
        for c in range(chunks)
    ]
    for copy in copies:
        copy.start()
    for c, copy in enumerate(copies):
        copy.wait()
        part = u_ref[pl.ds(c * step, step), :]
        product = bf_dot(part, part, TN)
        gram_ref[...] = product if c == 0 else gram_ref[...] + product

    tiles = modes // TILE
    inv_ref[...] = jnp.zeros_like(inv_ref)

    def one_tile(b, carry):
        base = pl.multiple_of(b * TILE, TILE)
        here = pl.ds(base, TILE)
        tile = gram_ref[here, here]
        sub = lax.broadcasted_iota(jnp.int32, (ROWS, TILE), 0)
        col = lax.broadcasted_iota(jnp.int32, (ROWS, TILE), 1)
        a_rows = [tile[ROWS * g : ROWS * (g + 1), :] for g in range(TILE // ROWS)]
        x_rows = [(col == sub + ROWS * g).astype(F32) for g in range(TILE // ROWS)]
        x_rows = factor_tile(a_rows, x_rows)
        for g in range(TILE // ROWS):
            x_ref[ROWS * g : ROWS * (g + 1), :] = x_rows[g]
        for static_b in range(tiles):

            @pl.when(b == static_b)
            def _():
                lo, hi = static_b * TILE, (static_b + 1) * TILE
                x = x_ref[...]
                inv_ref[lo:hi, lo:hi] = x
                if static_b:
                    inv_ref[lo:hi, :lo] = exact_dot(x, inv_ref[lo:hi, :lo], NN)
                if static_b + 1 < tiles:
                    upper = exact_dot(x, gram_ref[lo:hi, hi:], NN)
                    gram_ref[hi:, hi:] = gram_ref[hi:, hi:] - exact_dot(upper, upper, TN)
                    inv_ref[hi:, :hi] = inv_ref[hi:, :hi] - exact_dot(
                        upper, inv_ref[lo:hi, :hi], TN
                    )

        return carry

    lax.fori_loop(0, tiles, one_tile, 0)
    factor = inv_ref[...].T.astype(BF16)
    f_ref[...] = factor
    surface = head_ref.shape[0]
    head_ref[...] = bf_dot(u_ref[:surface, :], factor, NN).astype(BF16)
    tail_ref[...] = bf_dot(u_ref[orbitals - surface :, :], factor, NN).astype(BF16)


def apply_blocks(acc_ref, source_ref, blocks_ref, rows_ref, cols_ref, row_base, unroll):
    acc_ref[...] = jnp.zeros_like(acc_ref)

    def some(q, carry):
        for t in range(unroll):
            j = q * unroll + t
            to = pl.multiple_of((rows_ref[j] - row_base) * TILE, TILE)
            at = pl.multiple_of(cols_ref[j] * TILE, TILE)
            product = bf_dot(blocks_ref[j], source_ref[pl.ds(at, TILE), :], NN)
            acc_ref[pl.ds(to, TILE), :] = acc_ref[pl.ds(to, TILE), :] + product
        return carry

    count = blocks_ref.shape[0]
    lax.fori_loop(0, count // unroll, some, 0)
    for j in range(count - count % unroll, count):
        some_j = j
        to = pl.multiple_of((rows_ref[some_j] - row_base) * TILE, TILE)
        at = pl.multiple_of(cols_ref[some_j] * TILE, TILE)
        product = bf_dot(blocks_ref[some_j], source_ref[pl.ds(at, TILE), :], NN)
        acc_ref[pl.ds(to, TILE), :] = acc_ref[pl.ds(to, TILE), :] + product


def spread_kernel(rows_ref, cols_ref, u_ref, blocks_ref, order_ref, out_ref, acc_ref):
    apply_blocks(acc_ref, u_ref, blocks_ref, rows_ref, cols_ref, 0, 4)
    out_ref[...] = acc_ref[...].astype(BF16)


def couple_kernel(
    row_base, rows_ref, cols_ref, next_ref, blocks_ref, tail_ref, order_ref, right_ref, left_ref, acc_ref
):
    apply_blocks(acc_ref, next_ref, blocks_ref, rows_ref, cols_ref, row_base, 4)
    couple = bf_dot(tail_ref[...], acc_ref[...].astype(BF16), TN)
    right_ref[...] = couple
    left_ref[...] = couple.T


def split(value):
    high = value.astype(BF16)
    return high, (value - high.astype(F32)).astype(BF16)


def onsite_kernel(place_ref, u_ref, spread_ref, f_ref, steps_ref, order_ref, out_ref):
    modes = f_ref.shape[0]
    w = bf_dot(u_ref[...], spread_ref[...], TN)
    w = w + w.T
    f = f_ref[...]
    high, low = split(w)
    half = bf_dot(high, f, NN) + bf_dot(low, f, NN)
    high, low = split(half)
    full = bf_dot(f, high, TN) + bf_dot(f, low, TN)
    steps = steps_ref[...]
    reached = lax.broadcasted_iota(jnp.int32, steps.shape, 0) <= place_ref[0]
    potential = jnp.sum(jnp.where(reached, steps, 0.0), axis=0, keepdims=True)[:, :1]
    i = lax.broadcasted_iota(jnp.int32, (modes, modes), 0)
    j = lax.broadcasted_iota(jnp.int32, (modes, modes), 1)
    out_ref[...] = full + jnp.where(i == j, potential, 0.0)


def struct(shape, dtype):
    return jax.ShapeDtypeStruct(shape, dtype)


ANY = pl.BlockSpec(memory_space=pl.ANY)
INTO_VMEM = pl.BlockSpec(memory_space=pltpu.VMEM)
INTO_SMEM = pl.BlockSpec(memory_space=pltpu.SMEM)
PARAMS = pltpu.CompilerParams(vmem_limit_bytes=VMEM_LIMIT)


def passed_along(block, axis, distance):
    devices = range(lax.axis_size(axis))
    route = [(i - distance, i) for i in devices if i - distance in devices]
    return lax.ppermute(block, axis, route)


def cost(flops, moved):
    return pl.CostEstimate(flops=flops, bytes_accessed=moved, transcendentals=0)


def shards(
    trial_modes,
    onsite_blocks,
    onsite_rows,
    onsite_cols,
    coupling_blocks,
    coupling_rows,
    coupling_cols,
    potential_step,
):
    u = trial_modes[0]
    orbitals, modes = u.shape
    surface = SURFACE * TILE
    count = onsite_blocks.shape[1]
    links = coupling_blocks.shape[1]
    steps = lax.all_gather(
        lax.optimization_barrier(jnp.broadcast_to(potential_step[:, None], (1, TILE))),
        "slab",
        tiled=True,
    )
    place = lax.axis_index("slab").astype(jnp.int32).reshape(1)

    factor, head, tail = pl.pallas_call(
        factor_kernel,
        out_shape=(
            struct((modes, modes), BF16),
            struct((surface, modes), BF16),
            struct((surface, modes), BF16),
        ),
        in_specs=[ANY],
        out_specs=(INTO_VMEM,) * 3,
        scratch_shapes=[
            pltpu.VMEM((orbitals, modes), BF16),
            pltpu.VMEM((modes, modes), F32),
            pltpu.VMEM((modes, modes), F32),
            pltpu.VMEM((TILE, TILE), F32),
            pltpu.SemaphoreType.DMA((8,)),
        ],
        compiler_params=PARAMS,
        cost_estimate=cost(2 * orbitals * modes * modes, orbitals * modes * 2),
        name="factor",
    )(u)
    incoming = passed_along(head, "slab", -1)

    spread = pl.pallas_call(
        spread_kernel,
        out_shape=struct((orbitals, modes), BF16),
        in_specs=[INTO_SMEM, INTO_SMEM, INTO_VMEM, INTO_VMEM, ANY],
        out_specs=INTO_VMEM,
        scratch_shapes=[pltpu.VMEM((orbitals, modes), F32)],
        compiler_params=PARAMS,
        cost_estimate=cost(2 * count * TILE * TILE * modes, 3 * orbitals * modes * 2),
        name="spread",
    )(onsite_rows[0], onsite_cols[0], u, onsite_blocks[0], factor)

    right, left = pl.pallas_call(
        functools.partial(couple_kernel, orbitals // TILE - SURFACE),
        out_shape=(struct((modes, modes), F32),) * 2,
        in_specs=[INTO_SMEM, INTO_SMEM, INTO_VMEM, INTO_VMEM, INTO_VMEM, ANY],
        out_specs=(INTO_VMEM,) * 2,
        scratch_shapes=[pltpu.VMEM((surface, modes), F32)],
        compiler_params=PARAMS,
        cost_estimate=cost(2 * links * TILE * TILE * modes, 4 * surface * modes * 2),
        name="couple",
    )(coupling_rows[0], coupling_cols[0], incoming, coupling_blocks[0], tail, spread)
    coupling_left = passed_along(left, "slab", 1)

    onsite = pl.pallas_call(
        onsite_kernel,
        out_shape=struct((modes, modes), F32),
        in_specs=[INTO_SMEM, INTO_VMEM, INTO_VMEM, INTO_VMEM, INTO_VMEM, ANY],
        out_specs=INTO_VMEM,
        compiler_params=PARAMS,
        cost_estimate=cost(2 * orbitals * modes * modes, 2 * orbitals * modes * 2),
        name="onsite",
    )(place, u, spread, factor, steps, right)
    return (onsite[None], right[None], coupling_left[None])


def solution(mesh):
    return jax.shard_map(
        shards,
        mesh=mesh,
        in_specs=(
            P(("groups", "slab"), None, None),
            P(("groups", "slab"), None, None, None),
            P(("groups", "slab"), None),
            P(("groups", "slab"), None),
            P(("groups", "slab"), None, None, None),
            P(("groups", "slab"), None),
            P(("groups", "slab"), None),
            P(("groups", "slab")),
        ),
        out_specs=(
            P(("groups", "slab"), None, None),
            P(("groups", "slab"), None, None),
            P(("groups", "slab"), None, None),
        ),
        check_vma=False,
    )
```

```python
import functools

import jax
import jax.numpy as jnp
from jax import lax
from jax.experimental import pallas as pl
from jax.experimental.pallas import tpu as pltpu
from jax.sharding import PartitionSpec as P

F32 = jnp.float32
BF16 = jnp.bfloat16
VMEM_LIMIT = 56 * 1024 * 1024
SURFACE = 4
TILE = 128
ROWS = 8
COPIES = 64


def lane(value, k):
    return jnp.broadcast_to(value[:, k : k + 1], value.shape)


def row(value, k):
    return jnp.broadcast_to(value[k : k + 1, :], value.shape)


def exact_dot(a, b, dims):
    return lax.dot_general(
        a, b, (dims, ((), ())), precision=lax.Precision.HIGHEST, preferred_element_type=F32
    )


def bf_dot(a, b, dims):
    return lax.dot_general(a, b, (dims, ((), ())), preferred_element_type=F32)


NN = ((1,), (0,))
TN = ((0,), (0,))
NT = ((1,), (1,))


def factor_tile(a_rows, x_rows, between):
    panels = len(a_rows)
    for g in range(panels):
        here, here_x = a_rows[g], x_rows[g]
        columns = [lane(here, ROWS * g + j) for j in range(ROWS)]
        s = {(i, j): row(columns[j], i) for j in range(ROWS) for i in range(j, ROWS)}
        r = []
        for k in range(ROWS):
            r.append(lax.rsqrt(s[k, k]))
            for i in range(k + 1, ROWS):
                s[i, k] = s[i, k] * r[k]
            for j in range(k + 1, ROWS):
                for i in range(j, ROWS):
                    s[i, j] = s[i, j] - s[i, k] * s[j, k]
        z, zx = [], []
        for k in range(ROWS):
            top, top_x = row(here, k), row(here_x, k)
            for m in range(k):
                top = top - s[k, m] * z[m]
                top_x = top_x - s[k, m] * zx[m]
            z.append(top * r[k])
            zx.append(top_x * r[k])
        sub = lax.broadcasted_iota(jnp.int32, here.shape, 0)
        packed_x = zx[0]
        for k in range(1, ROWS):
            packed_x = jnp.where(sub == k, zx[k], packed_x)
        x_rows[g] = packed_x
        for i in range(g + 1, panels):
            below = []
            for k in range(ROWS):
                c = lane(a_rows[i], ROWS * g + k)
                for m in range(k):
                    c = c - below[m] * s[k, m]
                below.append(c * r[k])
            a_rows[i] = a_rows[i] - sum(below[k] * z[k] for k in range(ROWS))
            x_rows[i] = x_rows[i] - sum(below[k] * zx[k] for k in range(ROWS))
        between(g)
    return x_rows


def gram_kernel(u_hbm, gram_ref, u_ref, sems):
    chunks = sems.shape[0]
    step = u_ref.shape[0] // chunks
    copies = [
        pltpu.make_async_copy(
            u_hbm.at[pl.ds(c * step, step)], u_ref.at[pl.ds(c * step, step)], sems.at[c]
        )
        for c in range(chunks)
    ]
    for copy in copies:
        copy.start()
    for c, copy in enumerate(copies):
        copy.wait()
        part = u_ref[pl.ds(c * step, step), :]
        product = bf_dot(part, part, TN)
        gram_ref[...] = product if c == 0 else gram_ref[...] + product


def add_product(j, live, acc_ref, source_ref, blocks_ref, rows_ref, cols_ref, row_base):
    to = pl.multiple_of((rows_ref[j] - row_base) * TILE, TILE)
    at = pl.multiple_of(cols_ref[j] * TILE, TILE)
    product = bf_dot(blocks_ref[j], source_ref[pl.ds(at, TILE), :], NN)
    if live is not None:
        product = jnp.where(live, product, 0.0)
    acc_ref[pl.ds(to, TILE), :] = acc_ref[pl.ds(to, TILE), :] + product


def factor_kernel(
    rows_ref,
    cols_ref,
    crows_ref,
    ccols_ref,
    gram_in,
    next_ref,
    u_hbm,
    blocks_hbm,
    cblocks_hbm,
    f_ref,
    yt_ref,
    spread_hbm,
    gram_ref,
    inv_ref,
    x_ref,
    u_ref,
    blocks_ref,
    cblocks_ref,
    acc_ref,
    spread_ref,
    hop_ref,
    sems,
):
    orbitals, modes = u_ref.shape
    surface = hop_ref.shape[0]
    copies = [
        pltpu.make_async_copy(u_hbm, u_ref, sems.at[0]),
        pltpu.make_async_copy(blocks_hbm, blocks_ref, sems.at[1]),
        pltpu.make_async_copy(cblocks_hbm, cblocks_ref, sems.at[2]),
    ]
    for copy in copies:
        copy.start()
    acc_ref[...] = jnp.zeros_like(acc_ref)
    hop_ref[...] = jnp.zeros_like(hop_ref)
    inv_ref[...] = jnp.zeros_like(inv_ref)
    gram_ref[...] = gram_in[...]
    for copy in copies:
        copy.wait()

    tiles = modes // TILE
    panels = TILE // ROWS

    def onsite_product(j, live):
        add_product(j, live, acc_ref, u_ref, blocks_ref, rows_ref, cols_ref, 0)

    def coupling_product(j, live):
        base = (orbitals - surface) // TILE
        add_product(j, live, hop_ref, next_ref, cblocks_ref, crows_ref, ccols_ref, base)

    def one_tile(b, carry):
        here = pl.ds(pl.multiple_of(b * TILE, TILE), TILE)
        tile = gram_ref[here, here]
        sub = lax.broadcasted_iota(jnp.int32, (ROWS, TILE), 0)
        col = lax.broadcasted_iota(jnp.int32, (ROWS, TILE), 1)
        a_rows = [tile[ROWS * g : ROWS * (g + 1), :] for g in range(panels)]
        x_rows = [(col == sub + ROWS * g).astype(F32) for g in range(panels)]

        def between(g):
            for count, work in (
                (blocks_ref.shape[0], onsite_product),
                (cblocks_ref.shape[0], coupling_product),
            ):
                share = -(-count // tiles)
                for t in range(share):
                    if t * panels // share == g:
                        j = b * share + t
                        if share * tiles == count:
                            work(j, None)
                        else:
                            work(jnp.minimum(j, count - 1), j < count)

        x_rows = factor_tile(a_rows, x_rows, between)
        for g in range(panels):
            x_ref[ROWS * g : ROWS * (g + 1), :] = x_rows[g]
        for static_b in range(tiles):

            @pl.when(b == static_b)
            def _():
                lo, hi = static_b * TILE, (static_b + 1) * TILE
                x = x_ref[...]
                inv_ref[lo:hi, lo:hi] = x
                if static_b:
                    inv_ref[lo:hi, :lo] = exact_dot(x, inv_ref[lo:hi, :lo], NN)
                if static_b + 1 < tiles:
                    upper = exact_dot(x, gram_ref[lo:hi, hi:], NN)
                    gram_ref[hi:, hi:] = gram_ref[hi:, hi:] - exact_dot(upper, upper, TN)
                    inv_ref[hi:, :hi] = inv_ref[hi:, :hi] - exact_dot(
                        upper, inv_ref[lo:hi, :hi], TN
                    )

        return carry

    lax.fori_loop(0, tiles, one_tile, 0)
    spread_ref[...] = acc_ref[...].astype(BF16)
    out = pltpu.make_async_copy(spread_ref, spread_hbm, sems.at[3])
    out.start()
    factor = inv_ref[...].T.astype(BF16)
    f_ref[...] = factor
    high, low = split(bf_dot(u_ref[orbitals - surface :, :], hop_ref[...].astype(BF16), TN))
    yt_ref[...] = (bf_dot(high, factor, TN) + bf_dot(low, factor, TN)).astype(BF16)
    out.wait()


def couple_kernel(yt_ref, next_f_ref, f_ref, last_yt_ref, order_ref, right_ref, left_ref):
    right_ref[...] = bf_dot(yt_ref[...], next_f_ref[...], TN)
    left_ref[...] = bf_dot(f_ref[...], last_yt_ref[...], TN)


def split(value):
    high = value.astype(BF16)
    return high, (value - high.astype(F32)).astype(BF16)


def onsite_kernel(place_ref, u_hbm, spread_hbm, f_ref, steps_ref, out_ref, u_ref, spread_ref, w_ref, sems):
    modes = f_ref.shape[0]
    chunks = sems.shape[0]
    step = u_ref.shape[0] // chunks
    copies = []
    for c in range(chunks):
        part = pl.ds(c * step, step)
        copies.append(
            [
                pltpu.make_async_copy(u_hbm.at[part], u_ref.at[part], sems.at[c, 0]),
                pltpu.make_async_copy(spread_hbm.at[part], spread_ref.at[part], sems.at[c, 1]),
            ]
        )
    for pair in copies:
        for copy in pair:
            copy.start()
    for c, pair in enumerate(copies):
        for copy in pair:
            copy.wait()
        part = pl.ds(c * step, step)
        product = bf_dot(u_ref[part, :], spread_ref[part, :], TN)
        w_ref[...] = product if c == 0 else w_ref[...] + product
    w = w_ref[...]
    w = w + w.T
    f = f_ref[...]
    high, low = split(w)
    half = bf_dot(high, f, NN) + bf_dot(low, f, NN)
    high, low = split(half)
    full = bf_dot(f, high, TN) + bf_dot(f, low, TN)
    steps = steps_ref[...]
    index = lax.broadcasted_iota(jnp.int32, steps.shape, 0)
    used = (index <= place_ref[0] * COPIES) & (index % COPIES == 0)
    potential = jnp.sum(jnp.where(used, steps, 0.0), axis=0, keepdims=True)[:, :1]
    i = lax.broadcasted_iota(jnp.int32, (modes, modes), 0)
    j = lax.broadcasted_iota(jnp.int32, (modes, modes), 1)
    out_ref[...] = full + jnp.where(i == j, potential, 0.0)


def struct(shape, dtype):
    return jax.ShapeDtypeStruct(shape, dtype)


ANY = pl.BlockSpec(memory_space=pl.ANY)
INTO_VMEM = pl.BlockSpec(memory_space=pltpu.VMEM)
INTO_SMEM = pl.BlockSpec(memory_space=pltpu.SMEM)
PARAMS = pltpu.CompilerParams(vmem_limit_bytes=VMEM_LIMIT)


def passed_along(block, axis, distance):
    devices = range(lax.axis_size(axis))
    route = [(i - distance, i) for i in devices if i - distance in devices]
    return lax.ppermute(block, axis, route)


def cost(flops, moved):
    return pl.CostEstimate(flops=flops, bytes_accessed=moved, transcendentals=0)


def shards(
    trial_modes,
    onsite_blocks,
    onsite_rows,
    onsite_cols,
    coupling_blocks,
    coupling_rows,
    coupling_cols,
    potential_step,
):
    u = trial_modes[0]
    orbitals, modes = u.shape
    surface = SURFACE * TILE
    count = onsite_blocks.shape[1]
    links = coupling_blocks.shape[1]
    steps = lax.all_gather(
        lax.optimization_barrier(jnp.broadcast_to(potential_step[:, None], (COPIES, TILE))),
        "slab",
        tiled=True,
    )
    place = lax.axis_index("slab").astype(jnp.int32).reshape(1)
    next_head = passed_along(u[:surface], "slab", -1)

    gram = pl.pallas_call(
        gram_kernel,
        out_shape=struct((modes, modes), F32),
        in_specs=[ANY],
        out_specs=INTO_VMEM,
        scratch_shapes=[pltpu.VMEM((orbitals, modes), BF16), pltpu.SemaphoreType.DMA((8,))],
        compiler_params=PARAMS,
        cost_estimate=cost(2 * orbitals * modes * modes, orbitals * modes * 2),
        name="gram",
    )(u)

    factor, yt, spread = pl.pallas_call(
        factor_kernel,
        out_shape=(
            struct((modes, modes), BF16),
            struct((modes, modes), BF16),
            struct((orbitals, modes), BF16),
        ),
        in_specs=[INTO_SMEM] * 4 + [INTO_VMEM] * 2 + [ANY] * 3,
        out_specs=(INTO_VMEM, INTO_VMEM, ANY),
        scratch_shapes=[
            pltpu.VMEM((modes, modes), F32),
            pltpu.VMEM((modes, modes), F32),
            pltpu.VMEM((TILE, TILE), F32),
            pltpu.VMEM((orbitals, modes), BF16),
            pltpu.VMEM((count, TILE, TILE), BF16),
            pltpu.VMEM((links, TILE, TILE), BF16),
            pltpu.VMEM((orbitals, modes), F32),
            pltpu.VMEM((orbitals, modes), BF16),
            pltpu.VMEM((surface, modes), F32),
            pltpu.SemaphoreType.DMA((4,)),
        ],
        compiler_params=PARAMS,
        cost_estimate=cost(8 * orbitals * modes * modes, orbitals * modes * 2),
        name="factor",
    )(
        onsite_rows[0],
        onsite_cols[0],
        coupling_rows[0],
        coupling_cols[0],
        gram,
        next_head,
        u,
        onsite_blocks[0],
        coupling_blocks[0],
    )
    next_factor = passed_along(factor, "slab", -1)
    last_yt = passed_along(yt, "slab", 1)

    onsite = pl.pallas_call(
        onsite_kernel,
        out_shape=struct((modes, modes), F32),
        in_specs=[INTO_SMEM, ANY, ANY, INTO_VMEM, INTO_VMEM],
        out_specs=INTO_VMEM,
        scratch_shapes=[
            pltpu.VMEM((orbitals, modes), BF16),
            pltpu.VMEM((orbitals, modes), BF16),
            pltpu.VMEM((modes, modes), F32),
            pltpu.SemaphoreType.DMA((8, 2)),
        ],
        compiler_params=PARAMS,
        cost_estimate=cost(8 * modes * modes * modes, 8 * modes * modes * 2),
        name="onsite",
    )(place, u, spread, factor, steps)

    right, left = pl.pallas_call(
        couple_kernel,
        out_shape=(struct((modes, modes), F32),) * 2,
        in_specs=[INTO_VMEM] * 4 + [ANY],
        out_specs=(INTO_VMEM,) * 2,
        compiler_params=PARAMS,
        cost_estimate=cost(4 * modes * modes * modes, 8 * modes * modes * 2),
        name="couple",
    )(yt, next_factor, factor, last_yt, onsite)
    return (onsite[None], right[None], left[None])


def solution(mesh):
    return jax.shard_map(
        shards,
        mesh=mesh,
        in_specs=(
            P(("groups", "slab"), None, None),
            P(("groups", "slab"), None, None, None),
            P(("groups", "slab"), None),
            P(("groups", "slab"), None),
            P(("groups", "slab"), None, None, None),
            P(("groups", "slab"), None),
            P(("groups", "slab"), None),
            P(("groups", "slab")),
        ),
        out_specs=(
            P(("groups", "slab"), None, None),
            P(("groups", "slab"), None, None),
            P(("groups", "slab"), None, None),
        ),
        check_vma=False,
    )
```

```python
import functools

import jax
import jax.numpy as jnp
from jax import lax
from jax.experimental import pallas as pl
from jax.experimental.pallas import tpu as pltpu
from jax.sharding import PartitionSpec as P

F32 = jnp.float32
BF16 = jnp.bfloat16
MIB = 1024 * 1024
SURFACE = 4
TILE = 128
ROWS = 8


def lane(value, k):
    return jnp.broadcast_to(value[:, k : k + 1], value.shape)


def row(value, k):
    return jnp.broadcast_to(value[k : k + 1, :], value.shape)


def exact_dot(a, b, dims):
    return lax.dot_general(
        a, b, (dims, ((), ())), precision=lax.Precision.HIGHEST, preferred_element_type=F32
    )


def bf_dot(a, b, dims):
    return lax.dot_general(a, b, (dims, ((), ())), preferred_element_type=F32)


NN = ((1,), (0,))
TN = ((0,), (0,))
NT = ((1,), (1,))


def factor_tile(a_rows, x_rows, between):
    panels = len(a_rows)
    for g in range(panels):
        here, here_x = a_rows[g], x_rows[g]
        columns = [lane(here, ROWS * g + j) for j in range(ROWS)]
        s = {(i, j): row(columns[j], i) for j in range(ROWS) for i in range(j, ROWS)}
        low, r = {}, []
        for p in range(0, ROWS, 2):
            q = p + 1
            a, b, c = s[p, p], s[q, p], s[q, q]
            root = lax.rsqrt(a * c - b * b)
            r_p = lax.rsqrt(a)
            r_q = a * r_p * root
            inverse = root * root
            r += [r_p, r_q]
            low[q, p] = b * r_p
            side = {}
            for i in range(q + 1, ROWS):
                first, second = s[i, p], s[i, q]
                low[i, p] = first * r_p
                low[i, q] = (second - low[i, p] * low[q, p]) * r_q
                side[i] = (c * first - b * second, a * second - b * first)
            for j in range(q + 1, ROWS):
                for i in range(j, ROWS):
                    both = side[j][0] * s[i, p] + side[j][1] * s[i, q]
                    s[i, j] = s[i, j] - both * inverse
        z, zx = [], []
        for k in range(ROWS):
            top, top_x = row(here, k), row(here_x, k)
            for m in range(k):
                top = top - low[k, m] * z[m]
                top_x = top_x - low[k, m] * zx[m]
            z.append(top * r[k])
            zx.append(top_x * r[k])
        sub = lax.broadcasted_iota(jnp.int32, here.shape, 0)
        packed, packed_x = z[0], zx[0]
        for k in range(1, ROWS):
            packed = jnp.where(sub == k, z[k], packed)
            packed_x = jnp.where(sub == k, zx[k], packed_x)
        x_rows[g] = packed_x
        if g + 2 < panels:
            turned = packed.T
        for i in range(g + 1, panels):
            below = []
            for k in range(ROWS):
                if i == g + 1:
                    column = lane(a_rows[i], ROWS * g + k)
                    for m in range(k):
                        column = column - below[m] * low[k, m]
                    below.append(column * r[k])
                else:
                    below.append(
                        jnp.broadcast_to(turned[ROWS * i : ROWS * (i + 1), k : k + 1], here.shape)
                    )
            for k in range(ROWS):
                a_rows[i] = a_rows[i] - below[k] * z[k]
                x_rows[i] = x_rows[i] - below[k] * zx[k]
        between(g)
    return x_rows


def add_product(j, live, acc_ref, source_ref, blocks_ref, rows_ref, cols_ref, row_base):
    to = pl.multiple_of((rows_ref[j] - row_base) * TILE, TILE)
    at = pl.multiple_of(cols_ref[j] * TILE, TILE)
    product = bf_dot(blocks_ref[j], source_ref[pl.ds(at, TILE), :], NN)
    if live is not None:
        product = jnp.where(live, product, 0.0)
    acc_ref[pl.ds(to, TILE), :] = acc_ref[pl.ds(to, TILE), :] + product


def factor_kernel(
    rows_ref,
    cols_ref,
    u_hbm,
    blocks_hbm,
    f_ref,
    turned_hbm,
    spread_hbm,
    gram_ref,
    inv_ref,
    x_ref,
    u_ref,
    turned_ref,
    blocks_ref,
    acc_ref,
    spread_ref,
    sems,
    u_sems,
):
    orbitals, modes = u_ref.shape
    chunks = u_sems.shape[0]
    step = orbitals // chunks
    copies = [
        pltpu.make_async_copy(
            u_hbm.at[pl.ds(c * step, step)], u_ref.at[pl.ds(c * step, step)], u_sems.at[c]
        )
        for c in range(chunks)
    ]
    blocks_copy = pltpu.make_async_copy(blocks_hbm, blocks_ref, sems.at[0])
    for copy in copies:
        copy.start()
    blocks_copy.start()
    acc_ref[...] = jnp.zeros_like(acc_ref)
    inv_ref[...] = jnp.zeros_like(inv_ref)
    for c, copy in enumerate(copies):
        copy.wait()
        part = u_ref[c * step : (c + 1) * step, :]
        turned = part.T
        turned_ref[:, c * step : (c + 1) * step] = turned
        product = bf_dot(turned, part, NN)
        gram_ref[...] = product if c == 0 else gram_ref[...] + product
    turned_copy = pltpu.make_async_copy(turned_ref, turned_hbm, sems.at[1])
    turned_copy.start()
    gram = gram_ref[...]
    on_diagonal = lax.broadcasted_iota(jnp.int32, gram.shape, 0) == lax.broadcasted_iota(
        jnp.int32, gram.shape, 1
    )
    diagonal = jnp.where(on_diagonal, gram, 0.0)
    across = lax.rsqrt(jnp.sum(diagonal, axis=0, keepdims=True))
    down = lax.rsqrt(jnp.sum(diagonal, axis=1, keepdims=True))
    gram_ref[...] = gram * across * down
    blocks_copy.wait()

    tiles = modes // TILE
    panels = TILE // ROWS
    count = blocks_ref.shape[0]
    share = -(-count // tiles)

    def one_tile(b, carry):
        here = pl.ds(pl.multiple_of(b * TILE, TILE), TILE)
        tile = gram_ref[here, here]
        sub = lax.broadcasted_iota(jnp.int32, (ROWS, TILE), 0)
        col = lax.broadcasted_iota(jnp.int32, (ROWS, TILE), 1)
        a_rows = [tile[ROWS * g : ROWS * (g + 1), :] for g in range(panels)]
        x_rows = [(col == sub + ROWS * g).astype(F32) for g in range(panels)]

        def between(g):
            for t in range(share):
                if t * panels // share == g:
                    j = b * share + t
                    live = None
                    if share * tiles != count:
                        live = j < count
                        j = jnp.minimum(j, count - 1)
                    add_product(j, live, acc_ref, u_ref, blocks_ref, rows_ref, cols_ref, 0)

        x_rows = factor_tile(a_rows, x_rows, between)
        for g in range(panels):
            x_ref[ROWS * g : ROWS * (g + 1), :] = x_rows[g]
        for static_b in range(tiles):

            @pl.when(b == static_b)
            def _():
                lo, hi = static_b * TILE, (static_b + 1) * TILE
                x = x_ref[...]
                inv_ref[lo:hi, lo:hi] = x
                if static_b:
                    inv_ref[lo:hi, :lo] = exact_dot(x, inv_ref[lo:hi, :lo], NN)
                if static_b + 1 < tiles:
                    upper = exact_dot(x, gram_ref[lo:hi, hi:], NN)
                    gram_ref[hi:, hi:] = gram_ref[hi:, hi:] - exact_dot(upper, upper, TN)
                    inv_ref[hi:, :hi] = inv_ref[hi:, :hi] - exact_dot(
                        upper, inv_ref[lo:hi, :hi], TN
                    )

        return carry

    lax.fori_loop(0, tiles, one_tile, 0)
    spread_ref[...] = acc_ref[...].astype(BF16)
    spread_copy = pltpu.make_async_copy(spread_ref, spread_hbm, sems.at[2])
    spread_copy.start()
    f_ref[...] = (inv_ref[...] * across).T.astype(BF16)
    turned_copy.wait()
    spread_copy.wait()


def link_kernel(
    rows_ref, cols_ref, next_ref, blocks_ref, u_hbm, f_ref, yt_ref, hop_ref, tail_ref, sem
):
    surface = tail_ref.shape[0]
    base = u_hbm.shape[0] - surface
    copy = pltpu.make_async_copy(u_hbm.at[pl.ds(base, surface)], tail_ref, sem.at[0])
    copy.start()
    hop_ref[...] = jnp.zeros_like(hop_ref)
    for j in range(blocks_ref.shape[0]):
        add_product(j, None, hop_ref, next_ref, blocks_ref, rows_ref, cols_ref, base // TILE)
    copy.wait()
    high, low = split(bf_dot(tail_ref[...], hop_ref[...].astype(BF16), TN))
    factor = f_ref[...]
    yt_ref[...] = (bf_dot(high, factor, TN) + bf_dot(low, factor, TN)).astype(BF16)


def couple_kernel(yt_ref, next_f_ref, f_ref, last_yt_ref, order_ref, right_ref, left_ref):
    right_ref[...] = bf_dot(yt_ref[...], next_f_ref[...], TN)
    left_ref[...] = bf_dot(f_ref[...], last_yt_ref[...], TN)


def split(value):
    high = value.astype(BF16)
    return high, (value - high.astype(F32)).astype(BF16)


def onsite_kernel(
    place_ref, turned_hbm, spread_hbm, f_ref, steps_ref, order_ref, out_ref, turned_ref, spread_ref, w_ref, sems
):
    modes = f_ref.shape[0]
    chunks = sems.shape[0]
    step = spread_ref.shape[0] // chunks
    copies = []
    for c in range(chunks):
        part = pl.ds(c * step, step)
        copies.append(
            [
                pltpu.make_async_copy(turned_hbm.at[:, part], turned_ref.at[:, part], sems.at[c, 0]),
                pltpu.make_async_copy(spread_hbm.at[part], spread_ref.at[part], sems.at[c, 1]),
            ]
        )
    for pair in copies:
        for copy in pair:
            copy.start()
    for c, pair in enumerate(copies):
        for copy in pair:
            copy.wait()
        part = slice(c * step, (c + 1) * step)
        product = bf_dot(turned_ref[:, part], spread_ref[part, :], NN)
        w_ref[...] = product if c == 0 else w_ref[...] + product
    w = w_ref[...]
    w = w + w.T
    f = f_ref[...]
    high, low = split(w)
    half = bf_dot(high, f, NN) + bf_dot(low, f, NN)
    high, low = split(half)
    full = bf_dot(f, high, TN) + bf_dot(f, low, TN)
    steps = steps_ref[...]
    reached = lax.broadcasted_iota(jnp.int32, steps.shape, 0) <= place_ref[0]
    potential = jnp.sum(jnp.where(reached, steps, 0.0), axis=0, keepdims=True)[:, :1]
    i = lax.broadcasted_iota(jnp.int32, (modes, modes), 0)
    j = lax.broadcasted_iota(jnp.int32, (modes, modes), 1)
    out_ref[...] = full + jnp.where(i == j, potential, 0.0)


def struct(shape, dtype):
    return jax.ShapeDtypeStruct(shape, dtype)


ANY = pl.BlockSpec(memory_space=pl.ANY)
INTO_VMEM = pl.BlockSpec(memory_space=pltpu.VMEM)
INTO_SMEM = pl.BlockSpec(memory_space=pltpu.SMEM)


def params(mebibytes):
    return pltpu.CompilerParams(vmem_limit_bytes=mebibytes * MIB)


def passed_along(block, axis, distance):
    devices = range(lax.axis_size(axis))
    route = [(i - distance, i) for i in devices if i - distance in devices]
    return lax.ppermute(block, axis, route)


def cost(flops, moved):
    return pl.CostEstimate(flops=flops, bytes_accessed=moved, transcendentals=0)


def shards(
    trial_modes,
    onsite_blocks,
    onsite_rows,
    onsite_cols,
    coupling_blocks,
    coupling_rows,
    coupling_cols,
    potential_step,
):
    u = trial_modes[0]
    orbitals, modes = u.shape
    surface = SURFACE * TILE
    count = onsite_blocks.shape[1]
    links = coupling_blocks.shape[1]
    place = lax.axis_index("slab").astype(jnp.int32).reshape(1)
    next_head = passed_along(u[:surface], "slab", -1)
    slabs = lax.axis_size("slab")
    steps = lax.all_to_all(
        jnp.broadcast_to(potential_step[:, None], (slabs, TILE)), "slab", 0, 0, tiled=True
    )

    factor, turned, spread = pl.pallas_call(
        factor_kernel,
        out_shape=(
            struct((modes, modes), BF16),
            struct((modes, orbitals), BF16),
            struct((orbitals, modes), BF16),
        ),
        in_specs=[INTO_SMEM] * 2 + [ANY] * 2,
        out_specs=(INTO_VMEM, ANY, ANY),
        scratch_shapes=[
            pltpu.VMEM((modes, modes), F32),
            pltpu.VMEM((modes, modes), F32),
            pltpu.VMEM((TILE, TILE), F32),
            pltpu.VMEM((orbitals, modes), BF16),
            pltpu.VMEM((modes, orbitals), BF16),
            pltpu.VMEM((count, TILE, TILE), BF16),
            pltpu.VMEM((orbitals, modes), F32),
            pltpu.VMEM((orbitals, modes), BF16),
            pltpu.SemaphoreType.DMA((3,)),
            pltpu.SemaphoreType.DMA((8,)),
        ],
        compiler_params=params(56),
        cost_estimate=cost(8 * orbitals * modes * modes, orbitals * modes * 2),
        name="factor",
    )(onsite_rows[0], onsite_cols[0], u, onsite_blocks[0])
    next_factor = passed_along(factor, "slab", -1)

    yt = pl.pallas_call(
        link_kernel,
        out_shape=struct((modes, modes), BF16),
        in_specs=[INTO_SMEM] * 2 + [INTO_VMEM] * 2 + [ANY, INTO_VMEM],
        out_specs=INTO_VMEM,
        scratch_shapes=[
            pltpu.VMEM((surface, modes), F32),
            pltpu.VMEM((surface, modes), BF16),
            pltpu.SemaphoreType.DMA((1,)),
        ],
        compiler_params=params(12),
        cost_estimate=cost(2 * links * TILE * TILE * modes, 4 * surface * modes * 2),
        name="link",
    )(coupling_rows[0], coupling_cols[0], next_head, coupling_blocks[0], u, factor)
    last_yt = passed_along(yt, "slab", 1)

    onsite = pl.pallas_call(
        onsite_kernel,
        out_shape=struct((modes, modes), F32),
        in_specs=[INTO_SMEM, ANY, ANY, INTO_VMEM, INTO_VMEM, ANY],
        out_specs=INTO_VMEM,
        scratch_shapes=[
            pltpu.VMEM((modes, orbitals), BF16),
            pltpu.VMEM((orbitals, modes), BF16),
            pltpu.VMEM((modes, modes), F32),
            pltpu.SemaphoreType.DMA((8, 2)),
        ],
        compiler_params=params(24),
        cost_estimate=cost(8 * orbitals * modes * modes, 4 * orbitals * modes),
        name="onsite",
    )(place, turned, spread, factor, steps, yt)

    right, left = pl.pallas_call(
        couple_kernel,
        out_shape=(struct((modes, modes), F32),) * 2,
        in_specs=[INTO_VMEM] * 4 + [ANY],
        out_specs=(INTO_VMEM,) * 2,
        compiler_params=params(8),
        cost_estimate=cost(4 * modes * modes * modes, 8 * modes * modes * 2),
        name="couple",
    )(yt, next_factor, factor, last_yt, onsite)
    return (onsite[None], right[None], left[None])


def solution(mesh):
    return jax.shard_map(
        shards,
        mesh=mesh,
        in_specs=(
            P(("groups", "slab"), None, None),
            P(("groups", "slab"), None, None, None),
            P(("groups", "slab"), None),
            P(("groups", "slab"), None),
            P(("groups", "slab"), None, None, None),
            P(("groups", "slab"), None),
            P(("groups", "slab"), None),
            P(("groups", "slab")),
        ),
        out_specs=(
            P(("groups", "slab"), None, None),
            P(("groups", "slab"), None, None),
            P(("groups", "slab"), None, None),
        ),
        check_vma=False,
    )
```

```python
import functools

import jax
import jax.numpy as jnp
from jax import lax
from jax.experimental import pallas as pl
from jax.experimental.pallas import tpu as pltpu
from jax.sharding import PartitionSpec as P

F32 = jnp.float32
BF16 = jnp.bfloat16
VMEM_LIMIT = 63900000
SURFACE = 4
TILE = 128
ROWS = 8


def lane(value, k):
    return jnp.broadcast_to(value[:, k : k + 1], value.shape)


def row(ref, k, width):
    return jnp.broadcast_to(ref[k : k + 1, :], (ROWS, width))


def exact_dot(a, b, dims):
    return lax.dot_general(
        a, b, (dims, ((), ())), precision=lax.Precision.HIGHEST, preferred_element_type=F32
    )


def bf_dot(a, b, dims):
    return lax.dot_general(a, b, (dims, ((), ())), preferred_element_type=F32)


NN = ((1,), (0,))
TN = ((0,), (0,))
NT = ((1,), (1,))


def three_parts(value):
    a = value.astype(BF16).astype(F32)
    b = (value - a).astype(BF16).astype(F32)
    return a, b, value - a - b


def factor_tile(ax_ref, col_ref, between):
    width = ax_ref.shape[1]
    panels = ax_ref.shape[0] // ROWS
    near = 2
    for g in range(panels):
        base = ROWS * g
        here = ax_ref[base : base + ROWS, :TILE]
        for j in range(ROWS):
            col_ref[j] = lane(here, base + j)
        s = {(i, j): row(col_ref.at[j], i, TILE) for j in range(ROWS) for i in range(j, ROWS)}
        low, r = {}, []
        for p in range(0, ROWS, 2):
            q = p + 1
            a, b, c = s[p, p], s[q, p], s[q, q]
            root = lax.rsqrt(a * c - b * b)
            r_p = lax.rsqrt(a)
            r_q = a * r_p * root
            inverse = root * root
            r += [r_p, r_q]
            low[q, p] = b * r_p
            side = {}
            for i in range(q + 1, ROWS):
                first, second = s[i, p], s[i, q]
                low[i, p] = first * r_p
                low[i, q] = (second - low[i, p] * low[q, p]) * r_q
                side[i] = (c * first - b * second, a * second - b * first)
            for j in range(q + 1, ROWS):
                for i in range(j, ROWS):
                    both = side[j][0] * s[i, p] + side[j][1] * s[i, q]
                    s[i, j] = s[i, j] - both * inverse
        r2 = [jnp.concatenate([v, v], axis=1) for v in r]
        low2 = {key: jnp.concatenate([v, v], axis=1) for key, v in low.items()}
        z = []
        for k in range(ROWS):
            top = row(ax_ref, base + k, width)
            for m in range(k):
                top = top - low2[k, m] * z[m]
            z.append(top * r2[k])
        sub = lax.broadcasted_iota(jnp.int32, z[0].shape, 0)
        packed = z[0]
        for k in range(1, ROWS):
            packed = jnp.where(sub == k, z[k], packed)
        for i in range(g + 1, min(g + 1 + near, panels)):
            at = ROWS * i
            block = ax_ref[at : at + ROWS, :]
            below = []
            for k in range(ROWS):
                column = lane(block[:, :TILE], base + k)
                for m in range(k):
                    column = column - below[m] * low[k, m]
                below.append(column * r[k])
            for k in range(ROWS):
                block = block - jnp.concatenate([below[k], below[k]], axis=1) * z[k]
            ax_ref[at : at + ROWS, :] = block
        ax_ref[base : base + ROWS, TILE:] = packed[:, TILE:]
        far = ROWS * (g + 1 + near)
        if far < ax_ref.shape[0]:
            a, b, c = three_parts(packed)
            left = jnp.concatenate([v[:, :TILE] for v in (a, a, b, b, a, c)], axis=0).astype(BF16)
            right = jnp.concatenate([a, b, a, b, c, a], axis=0).astype(BF16)
            product = bf_dot(left, right, TN)
            ax_ref[far:, :] = ax_ref[far:, :] - product[far:, :]
        between(g)


def add_product(j, live, acc_ref, source_ref, blocks_ref, rows_ref, cols_ref, row_base):
    to = pl.multiple_of((rows_ref[j] - row_base) * TILE, TILE)
    at = pl.multiple_of(cols_ref[j] * TILE, TILE)
    product = bf_dot(blocks_ref[j], source_ref[pl.ds(at, TILE), :], NN)
    if live is not None:
        product = jnp.where(live, product, 0.0)
    acc_ref[pl.ds(to, TILE), :] = acc_ref[pl.ds(to, TILE), :] + product


def factor_kernel(
    rows_ref,
    cols_ref,
    u_hbm,
    blocks_hbm,
    f_ref,
    w_ref,
    gram_ref,
    upper_ref,
    inv_ref,
    ax_ref,
    col_ref,
    u_ref,
    turned_ref,
    blocks_ref,
    acc_ref,
    sems,
    u_sems,
):
    orbitals, modes = u_ref.shape
    tiles = modes // TILE
    panels = TILE // ROWS
    step = orbitals // panels
    chunks = u_sems.shape[0]
    long_step = orbitals // chunks
    copies = [
        pltpu.make_async_copy(
            u_hbm.at[pl.ds(c * long_step, long_step)],
            u_ref.at[pl.ds(c * long_step, long_step)],
            u_sems.at[c],
        )
        for c in range(chunks)
    ]
    blocks_copy = pltpu.make_async_copy(blocks_hbm, blocks_ref, sems.at[0])
    for copy in copies:
        copy.start()
    blocks_copy.start()
    acc_ref[...] = jnp.zeros_like(acc_ref)
    inv_ref[...] = jnp.zeros_like(inv_ref)
    upper_ref[...] = jnp.zeros_like(upper_ref)

    def gram_part(of, store, first, size):
        turned = u_ref[first : first + size, of].T
        turned_ref[store, first : first + size] = turned
        return bf_dot(turned, u_ref[first : first + size, :], NN)

    block0 = pl.ds(0, TILE)
    for c, copy in enumerate(copies):
        copy.wait()
        product = gram_part(block0, block0, c * long_step, long_step)
        gram_ref[0] = product if c == 0 else gram_ref[0] + product
    blocks_copy.wait()

    count = blocks_ref.shape[0]
    share = -(-count // tiles)

    def one_tile(b, carry):
        here = pl.ds(pl.multiple_of(b * TILE, TILE), TILE)
        later = pl.ds(pl.multiple_of(jnp.minimum(b + 1, tiles - 1) * TILE, TILE), TILE)
        store = pl.ds(pl.multiple_of((b + 1) * TILE, TILE), TILE)
        tile = gram_ref[0, :, here]
        on_diagonal = lax.broadcasted_iota(jnp.int32, tile.shape, 0) == lax.broadcasted_iota(
            jnp.int32, tile.shape, 1
        )
        diagonal = jnp.where(on_diagonal, tile, 0.0)
        across = lax.rsqrt(jnp.sum(diagonal, axis=0, keepdims=True))
        down = lax.rsqrt(jnp.sum(diagonal, axis=1, keepdims=True))
        ax_ref[:, :TILE] = tile * across * down
        ax_ref[:, TILE:] = on_diagonal.astype(F32)

        def between(g):
            product = gram_part(later, store, g * step, step)
            gram_ref[1] = product if g == 0 else gram_ref[1] + product
            for t in range(share):
                if t * panels // share == g:
                    j = b * share + t
                    live = None
                    if share * tiles != count:
                        live = j < count
                        j = jnp.minimum(j, count - 1)
                    add_product(j, live, acc_ref, u_ref, blocks_ref, rows_ref, cols_ref, 0)

        factor_tile(ax_ref, col_ref, between)
        x = ax_ref[:, TILE:] * across
        inv_part = exact_dot(upper_ref[:, here], inv_ref[...], TN)
        inv_ref[here, :] = -exact_dot(x, inv_part, NN)
        inv_ref[here, here] = x
        upper_ref[here, :] = exact_dot(x, gram_ref[0], NN)
        gram_ref[0] = gram_ref[1] - exact_dot(upper_ref[:, later], upper_ref[...], TN)
        return carry

    lax.fori_loop(0, tiles, one_tile, 0)
    f_ref[...] = inv_ref[...].T.astype(BF16)
    for c in range(chunks):
        part = slice(c * long_step, (c + 1) * long_step)
        product = bf_dot(turned_ref[:modes, part], acc_ref[part, :].astype(BF16), NN)
        w_ref[...] = product if c == 0 else w_ref[...] + product


def link_kernel(
    rows_ref,
    cols_ref,
    next_hbm,
    blocks_hbm,
    u_hbm,
    f_hbm,
    yt_ref,
    hop_ref,
    next_ref,
    blocks_ref,
    tail_ref,
    f_ref,
    sems,
):
    surface = tail_ref.shape[0]
    base = u_hbm.shape[0] - surface
    pairs = [
        (next_hbm, next_ref),
        (blocks_hbm, blocks_ref),
        (u_hbm.at[pl.ds(base, surface)], tail_ref),
        (f_hbm, f_ref),
    ]
    copies = [pltpu.make_async_copy(a, b, sems.at[n]) for n, (a, b) in enumerate(pairs)]
    for copy in copies:
        copy.start()
    hop_ref[...] = jnp.zeros_like(hop_ref)
    for copy in copies:
        copy.wait()
    for j in range(blocks_ref.shape[0]):
        add_product(j, None, hop_ref, next_ref, blocks_ref, rows_ref, cols_ref, base // TILE)
    high, low = split(bf_dot(tail_ref[...], hop_ref[...].astype(BF16), TN))
    factor = f_ref[...]
    yt_ref[...] = (bf_dot(high, factor, TN) + bf_dot(low, factor, TN)).astype(BF16)


def couple_kernel(yt_ref, next_f_ref, f_ref, last_yt_ref, order_ref, right_ref, left_ref):
    right_ref[...] = bf_dot(yt_ref[...], next_f_ref[...], TN)
    left_ref[...] = bf_dot(f_ref[...], last_yt_ref[...], TN)


def split(value):
    high = value.astype(BF16)
    return high, (value - high.astype(F32)).astype(BF16)


def onsite_kernel(place_ref, w_ref, f_ref, steps_ref, order_ref, out_ref, done_ref):
    modes = f_ref.shape[0]
    w = w_ref[...]
    w = w + w.T
    f = f_ref[...]
    high, low = split(w)
    half = bf_dot(high, f, NN) + bf_dot(low, f, NN)
    high, low = split(half)
    full = bf_dot(f, high, TN) + bf_dot(f, low, TN)
    steps = steps_ref[...]
    reached = lax.broadcasted_iota(jnp.int32, steps.shape, 0) <= place_ref[0]
    potential = jnp.sum(jnp.where(reached, steps, 0.0), axis=0, keepdims=True)[:, :1]
    i = lax.broadcasted_iota(jnp.int32, (modes, modes), 0)
    j = lax.broadcasted_iota(jnp.int32, (modes, modes), 1)
    out_ref[...] = full + jnp.where(i == j, potential, 0.0)
    done_ref[...] = jnp.zeros_like(done_ref)


def struct(shape, dtype):
    return jax.ShapeDtypeStruct(shape, dtype)


ANY = pl.BlockSpec(memory_space=pl.ANY)
INTO_VMEM = pl.BlockSpec(memory_space=pltpu.VMEM)
INTO_SMEM = pl.BlockSpec(memory_space=pltpu.SMEM)


PARAMS = pltpu.CompilerParams(vmem_limit_bytes=VMEM_LIMIT)
SMALL = pltpu.CompilerParams(vmem_limit_bytes=8 * 1024 * 1024)


def passed_along(block, axis, distance):
    devices = range(lax.axis_size(axis))
    route = [(i - distance, i) for i in devices if i - distance in devices]
    return lax.ppermute(block, axis, route)


def cost(flops, moved):
    return pl.CostEstimate(flops=flops, bytes_accessed=moved, transcendentals=0)


def shards(
    trial_modes,
    onsite_blocks,
    onsite_rows,
    onsite_cols,
    coupling_blocks,
    coupling_rows,
    coupling_cols,
    potential_step,
):
    u = trial_modes[0]
    orbitals, modes = u.shape
    surface = SURFACE * TILE
    count = onsite_blocks.shape[1]
    links = coupling_blocks.shape[1]
    place = lax.axis_index("slab").astype(jnp.int32).reshape(1)
    next_head = passed_along(u[:surface], "slab", -1)
    slabs = lax.axis_size("slab")
    steps = lax.all_to_all(
        jnp.broadcast_to(potential_step[:, None], (slabs, TILE)), "slab", 0, 0, tiled=True
    )

    factor, w = pl.pallas_call(
        factor_kernel,
        out_shape=(struct((modes, modes), BF16), struct((modes, modes), F32)),
        in_specs=[INTO_SMEM] * 2 + [ANY] * 2,
        out_specs=(INTO_VMEM,) * 2,
        scratch_shapes=[
            pltpu.VMEM((2, TILE, modes), F32),
            pltpu.VMEM((modes, modes), F32),
            pltpu.VMEM((modes, modes), F32),
            pltpu.VMEM((TILE, 2 * TILE), F32),
            pltpu.VMEM((ROWS, ROWS, TILE), F32),
            pltpu.VMEM((orbitals, modes), BF16),
            pltpu.VMEM((modes + TILE, orbitals), BF16),
            pltpu.VMEM((count, TILE, TILE), BF16),
            pltpu.VMEM((orbitals, modes), F32),
            pltpu.SemaphoreType.DMA((1,)),
            pltpu.SemaphoreType.DMA((8,)),
        ],
        compiler_params=PARAMS,
        cost_estimate=cost(8 * orbitals * modes * modes, orbitals * modes * 2),
        name="factor",
    )(onsite_rows[0], onsite_cols[0], u, onsite_blocks[0])
    next_factor = passed_along(factor, "slab", -1)

    yt = pl.pallas_call(
        link_kernel,
        out_shape=struct((modes, modes), BF16),
        in_specs=[INTO_SMEM] * 2 + [ANY] * 4,
        out_specs=INTO_VMEM,
        scratch_shapes=[
            pltpu.VMEM((surface, modes), F32),
            pltpu.VMEM((surface, modes), BF16),
            pltpu.VMEM((links, TILE, TILE), BF16),
            pltpu.VMEM((surface, modes), BF16),
            pltpu.VMEM((modes, modes), BF16),
            pltpu.SemaphoreType.DMA((4,)),
        ],
        compiler_params=PARAMS,
        cost_estimate=cost(2 * links * TILE * TILE * modes, 4 * surface * modes * 2),
        name="link",
    )(coupling_rows[0], coupling_cols[0], next_head, coupling_blocks[0], u, factor)
    last_yt = passed_along(yt, "slab", 1)

    onsite, done = pl.pallas_call(
        onsite_kernel,
        out_shape=(struct((modes, modes), F32), struct((ROWS, TILE), F32)),
        in_specs=[INTO_SMEM] + [INTO_VMEM] * 3 + [ANY],
        out_specs=(INTO_VMEM,) * 2,
        compiler_params=PARAMS,
        cost_estimate=cost(8 * orbitals * modes * modes, 4 * orbitals * modes),
        name="onsite",
    )(place, w, factor, steps, yt)

    right, left = pl.pallas_call(
        couple_kernel,
        out_shape=(struct((modes, modes), F32),) * 2,
        in_specs=[INTO_VMEM] * 4 + [ANY],
        out_specs=(INTO_VMEM,) * 2,
        compiler_params=SMALL,
        cost_estimate=cost(4 * modes * modes * modes, 8 * modes * modes * 2),
        name="couple",
    )(yt, next_factor, factor, last_yt, done)
    return (onsite[None], right[None], left[None])


def solution(mesh):
    return jax.shard_map(
        shards,
        mesh=mesh,
        in_specs=(
            P(("groups", "slab"), None, None),
            P(("groups", "slab"), None, None, None),
            P(("groups", "slab"), None),
            P(("groups", "slab"), None),
            P(("groups", "slab"), None, None, None),
            P(("groups", "slab"), None),
            P(("groups", "slab"), None),
            P(("groups", "slab")),
        ),
        out_specs=(
            P(("groups", "slab"), None, None),
            P(("groups", "slab"), None, None),
            P(("groups", "slab"), None, None),
        ),
        check_vma=False,
    )
```

```python
import functools

import jax
import jax.numpy as jnp
from jax import lax
from jax.experimental import pallas as pl
from jax.experimental.pallas import tpu as pltpu
from jax.sharding import PartitionSpec as P

F32 = jnp.float32
BF16 = jnp.bfloat16
VMEM_LIMIT = 63900000
SURFACE = 4
TILE = 128
ROWS = 8


def lane(value, k):
    return jnp.broadcast_to(value[:, k : k + 1], value.shape)


def row(ref, k, width):
    return jnp.broadcast_to(ref[k : k + 1, :], (ROWS, width))


def exact_dot(a, b, dims):
    return lax.dot_general(
        a, b, (dims, ((), ())), precision=lax.Precision.HIGHEST, preferred_element_type=F32
    )


def bf_dot(a, b, dims):
    return lax.dot_general(a, b, (dims, ((), ())), preferred_element_type=F32)


NN = ((1,), (0,))
TN = ((0,), (0,))
NT = ((1,), (1,))


def three_parts(value):
    a = value.astype(BF16).astype(F32)
    b = (value - a).astype(BF16).astype(F32)
    return a, b, value - a - b


def factor_tile(ax_ref, col_ref, between):
    width = ax_ref.shape[1]
    panels = ax_ref.shape[0] // ROWS
    near = 2
    for g in range(panels):
        base = ROWS * g
        here = ax_ref[base : base + ROWS, :TILE]
        for j in range(ROWS):
            col_ref[j] = lane(here, base + j)
        s = {(i, j): row(col_ref.at[j], i, TILE) for j in range(ROWS) for i in range(j, ROWS)}
        low, r = {}, []
        for p in range(0, ROWS, 2):
            q = p + 1
            a, b, c = s[p, p], s[q, p], s[q, q]
            root = lax.rsqrt(a * c - b * b)
            r_p = lax.rsqrt(a)
            r_q = a * r_p * root
            inverse = root * root
            r += [r_p, r_q]
            low[q, p] = b * r_p
            side = {}
            for i in range(q + 1, ROWS):
                first, second = s[i, p], s[i, q]
                low[i, p] = first * r_p
                low[i, q] = (second - low[i, p] * low[q, p]) * r_q
                side[i] = (c * first - b * second, a * second - b * first)
            for j in range(q + 1, ROWS):
                for i in range(j, ROWS):
                    both = side[j][0] * s[i, p] + side[j][1] * s[i, q]
                    s[i, j] = s[i, j] - both * inverse
        r2 = [jnp.concatenate([v, v], axis=1) for v in r]
        low2 = {key: jnp.concatenate([v, v], axis=1) for key, v in low.items()}
        z = []
        for k in range(ROWS):
            top = row(ax_ref, base + k, width)
            for m in range(k):
                top = top - low2[k, m] * z[m]
            z.append(top * r2[k])
        sub = lax.broadcasted_iota(jnp.int32, z[0].shape, 0)
        packed = z[0]
        for k in range(1, ROWS):
            packed = jnp.where(sub == k, z[k], packed)
        for i in range(g + 1, min(g + 1 + near, panels)):
            at = ROWS * i
            block = ax_ref[at : at + ROWS, :]
            below = []
            for k in range(ROWS):
                column = lane(block[:, :TILE], base + k)
                for m in range(k):
                    column = column - below[m] * low[k, m]
                below.append(column * r[k])
            for k in range(ROWS):
                block = block - jnp.concatenate([below[k], below[k]], axis=1) * z[k]
            ax_ref[at : at + ROWS, :] = block
        ax_ref[base : base + ROWS, TILE:] = packed[:, TILE:]
        far = ROWS * (g + 1 + near)
        if far < ax_ref.shape[0]:
            a, b, c = three_parts(packed)
            left = jnp.concatenate([v[:, :TILE] for v in (a, a, b, b, a, c)], axis=0).astype(BF16)
            right = jnp.concatenate([a, b, a, b, c, a], axis=0).astype(BF16)
            product = bf_dot(left, right, TN)
            ax_ref[far:, :] = ax_ref[far:, :] - product[far:, :]
        between(g)


def add_product(j, live, acc_ref, source_ref, blocks_ref, rows_ref, cols_ref, row_base):
    to = pl.multiple_of((rows_ref[j] - row_base) * TILE, TILE)
    at = pl.multiple_of(cols_ref[j] * TILE, TILE)
    product = bf_dot(blocks_ref[j], source_ref[pl.ds(at, TILE), :], NN)
    if live is not None:
        product = jnp.where(live, product, 0.0)
    acc_ref[pl.ds(to, TILE), :] = acc_ref[pl.ds(to, TILE), :] + product


def factor_kernel(
    rows_ref,
    cols_ref,
    crows_ref,
    ccols_ref,
    next_hbm,
    u_hbm,
    blocks_hbm,
    cblocks_hbm,
    f_ref,
    yt_ref,
    w_ref,
    gram_ref,
    upper_ref,
    inv_ref,
    ax_ref,
    col_ref,
    u_ref,
    turned_ref,
    blocks_ref,
    acc_ref,
    next_ref,
    cblocks_ref,
    hop_ref,
    m_ref,
    sems,
    u_sems,
):
    orbitals, modes = u_ref.shape
    surface = hop_ref.shape[0]
    tiles = modes // TILE
    panels = TILE // ROWS
    step = orbitals // panels
    chunks = u_sems.shape[0]
    long_step = orbitals // chunks
    copies = [
        pltpu.make_async_copy(
            u_hbm.at[pl.ds(c * long_step, long_step)],
            u_ref.at[pl.ds(c * long_step, long_step)],
            u_sems.at[c],
        )
        for c in range(chunks)
    ]
    more = [
        pltpu.make_async_copy(blocks_hbm, blocks_ref, sems.at[0]),
        pltpu.make_async_copy(cblocks_hbm, cblocks_ref, sems.at[1]),
        pltpu.make_async_copy(next_hbm, next_ref, sems.at[2]),
    ]
    for copy in copies + more:
        copy.start()
    acc_ref[...] = jnp.zeros_like(acc_ref)
    hop_ref[...] = jnp.zeros_like(hop_ref)
    inv_ref[...] = jnp.zeros_like(inv_ref)

    def tile_of(t):
        return slice(t * TILE, (t + 1) * TILE)

    def gram_part(lo, hi, first, size):
        piece = slice(first, first + size)
        turned = u_ref[piece, lo:hi].T
        turned_ref[lo:hi, piece] = turned
        product = bf_dot(turned, u_ref[piece, lo:], NN)
        if first == 0:
            gram_ref[lo:hi, lo:] = product
        else:
            gram_ref[lo:hi, lo:] = gram_ref[lo:hi, lo:] + product

    for c, copy in enumerate(copies):
        copy.wait()
        gram_part(0, TILE, c * long_step, long_step)
    for copy in more:
        copy.wait()

    def onsite_product(j):
        add_product(j, None, acc_ref, u_ref, blocks_ref, rows_ref, cols_ref, 0)

    def coupling_product(j):
        base = (orbitals - surface) // TILE
        add_product(j, None, hop_ref, next_ref, cblocks_ref, crows_ref, ccols_ref, base)

    def reduce_part(out_ref, base, source_ref, first):
        left = turned_ref[:, base + first : base + first + step]
        product = bf_dot(left, source_ref[first : first + step, :].astype(BF16), NN)
        out_ref[...] = product if first == 0 else out_ref[...] + product

    def schur(i, j, t):
        gram_ref[tile_of(i), tile_of(j)] = gram_ref[tile_of(i), tile_of(j)] - exact_dot(
            upper_ref[tile_of(t), tile_of(i)], upper_ref[tile_of(t), tile_of(j)], TN
        )

    def inverse_sum(i, t):
        width = slice(0, (t + 1) * TILE)
        inv_ref[tile_of(i), width] = inv_ref[tile_of(i), width] - exact_dot(
            upper_ref[tile_of(t), tile_of(i)], inv_ref[tile_of(t), width], TN
        )

    def inverse_row(i):
        width = slice(0, i * TILE)
        inv_ref[tile_of(i), width] = exact_dot(
            inv_ref[tile_of(i), tile_of(i)], inv_ref[tile_of(i), width], NN
        )

    call = functools.partial
    products = [call(onsite_product, j) for j in range(blocks_ref.shape[0])]
    products += [call(coupling_product, j) for j in range(cblocks_ref.shape[0])]
    reductions = [call(reduce_part, w_ref, 0, acc_ref, c * step) for c in range(panels)]
    reductions += [
        call(reduce_part, m_ref, orbitals - surface, hop_ref, first)
        for first in range(0, surface, step)
    ]
    plan = {(t, g): [] for t in range(tiles) for g in range(panels)}
    for g in range(panels):
        plan[0, g].append(call(gram_part, TILE, modes, g * step, step))
    room = [(t, g) for t in range(tiles - 1) for g in range(panels)]
    for n, work in enumerate(products):
        plan[room[n * len(room) // len(products)]].append(work)
    for n, work in enumerate(reductions):
        plan[tiles - 1, n * panels // len(reductions)].append(work)
    for t in range(1, tiles):
        late = []
        if t > 1:
            late.append(call(inverse_row, t - 1))
        late += [call(schur, i, j, t - 1) for i in range(t, tiles) for j in range(i, tiles)][1:]
        late += [call(inverse_sum, i, t - 1) for i in range(t, tiles)]
        for n, work in enumerate(late):
            plan[t, n * (panels - 2) // len(late)].insert(0, work)

    def one_tile(t):
        here = tile_of(t)
        tile = gram_ref[here, here]
        on_diagonal = lax.broadcasted_iota(jnp.int32, tile.shape, 0) == lax.broadcasted_iota(
            jnp.int32, tile.shape, 1
        )
        diagonal = jnp.where(on_diagonal, tile, 0.0)
        across = lax.rsqrt(jnp.sum(diagonal, axis=0, keepdims=True))
        down = lax.rsqrt(jnp.sum(diagonal, axis=1, keepdims=True))
        ax_ref[:, :TILE] = tile * across * down
        ax_ref[:, TILE:] = on_diagonal.astype(F32)

        def between(g):
            for work in plan[t, g]:
                work()

        factor_tile(ax_ref, col_ref, between)
        x = ax_ref[:, TILE:] * across
        inv_ref[here, here] = x
        if t + 1 < tiles:
            upper_ref[here, (t + 1) * TILE :] = exact_dot(x, gram_ref[here, (t + 1) * TILE :], NN)
            schur(t + 1, t + 1, t)
        else:
            inverse_row(t)

    def step_of(b, carry):
        for t in range(tiles):
            pl.when(b == t)(call(one_tile, t))
        return carry

    lax.fori_loop(0, tiles, step_of, 0)
    factor = inv_ref[...].T.astype(BF16)
    f_ref[...] = factor
    high, low = split(m_ref[...])
    yt_ref[...] = (bf_dot(high, factor, TN) + bf_dot(low, factor, TN)).astype(BF16)


def couple_kernel(yt_ref, next_f_ref, f_ref, last_yt_ref, order_ref, right_ref, left_ref):
    right_ref[...] = bf_dot(yt_ref[...], next_f_ref[...], TN)
    left_ref[...] = bf_dot(f_ref[...], last_yt_ref[...], TN)


def split(value):
    high = value.astype(BF16)
    return high, (value - high.astype(F32)).astype(BF16)


def onsite_kernel(place_ref, w_ref, f_ref, steps_ref, order_ref, out_ref, done_ref):
    modes = f_ref.shape[0]
    w = w_ref[...]
    w = w + w.T
    f = f_ref[...]
    high, low = split(w)
    half = bf_dot(high, f, NN) + bf_dot(low, f, NN)
    high, low = split(half)
    full = bf_dot(f, high, TN) + bf_dot(f, low, TN)
    steps = steps_ref[...]
    reached = lax.broadcasted_iota(jnp.int32, steps.shape, 0) <= place_ref[0]
    potential = jnp.sum(jnp.where(reached, steps, 0.0), axis=0, keepdims=True)[:, :1]
    i = lax.broadcasted_iota(jnp.int32, (modes, modes), 0)
    j = lax.broadcasted_iota(jnp.int32, (modes, modes), 1)
    out_ref[...] = full + jnp.where(i == j, potential, 0.0)
    done_ref[...] = jnp.zeros_like(done_ref)


def struct(shape, dtype):
    return jax.ShapeDtypeStruct(shape, dtype)


ANY = pl.BlockSpec(memory_space=pl.ANY)
INTO_VMEM = pl.BlockSpec(memory_space=pltpu.VMEM)
INTO_SMEM = pl.BlockSpec(memory_space=pltpu.SMEM)


PARAMS = pltpu.CompilerParams(vmem_limit_bytes=VMEM_LIMIT)
SMALL = pltpu.CompilerParams(vmem_limit_bytes=8 * 1024 * 1024)


def passed_along(block, axis, distance):
    devices = range(lax.axis_size(axis))
    route = [(i - distance, i) for i in devices if i - distance in devices]
    return lax.ppermute(block, axis, route)


def cost(flops, moved):
    return pl.CostEstimate(flops=flops, bytes_accessed=moved, transcendentals=0)


def shards(
    trial_modes,
    onsite_blocks,
    onsite_rows,
    onsite_cols,
    coupling_blocks,
    coupling_rows,
    coupling_cols,
    potential_step,
):
    u = trial_modes[0]
    orbitals, modes = u.shape
    surface = SURFACE * TILE
    count = onsite_blocks.shape[1]
    links = coupling_blocks.shape[1]
    place = lax.axis_index("slab").astype(jnp.int32).reshape(1)
    slabs = lax.axis_size("slab")
    next_head = passed_along(u[:surface], "slab", -1)
    steps = lax.all_to_all(
        jnp.broadcast_to(potential_step[:, None], (slabs, TILE)), "slab", 0, 0, tiled=True
    )

    factor, yt, w = pl.pallas_call(
        factor_kernel,
        out_shape=(
            struct((modes, modes), BF16),
            struct((modes, modes), BF16),
            struct((modes, modes), F32),
        ),
        in_specs=[INTO_SMEM] * 4 + [ANY] * 4,
        out_specs=(INTO_VMEM,) * 3,
        scratch_shapes=[
            pltpu.VMEM((modes, modes), F32),
            pltpu.VMEM((modes, modes), F32),
            pltpu.VMEM((modes, modes), F32),
            pltpu.VMEM((TILE, 2 * TILE), F32),
            pltpu.VMEM((ROWS, ROWS, TILE), F32),
            pltpu.VMEM((orbitals, modes), BF16),
            pltpu.VMEM((modes, orbitals), BF16),
            pltpu.VMEM((count, TILE, TILE), BF16),
            pltpu.VMEM((orbitals, modes), F32),
            pltpu.VMEM((surface, modes), BF16),
            pltpu.VMEM((links, TILE, TILE), BF16),
            pltpu.VMEM((surface, modes), F32),
            pltpu.VMEM((modes, modes), F32),
            pltpu.SemaphoreType.DMA((3,)),
            pltpu.SemaphoreType.DMA((8,)),
        ],
        compiler_params=PARAMS,
        cost_estimate=cost(8 * orbitals * modes * modes, orbitals * modes * 2),
        name="factor",
    )(
        onsite_rows[0],
        onsite_cols[0],
        coupling_rows[0],
        coupling_cols[0],
        next_head,
        u,
        onsite_blocks[0],
        coupling_blocks[0],
    )
    next_factor = passed_along(factor, "slab", -1)
    last_yt = passed_along(yt, "slab", 1)

    onsite, done = pl.pallas_call(
        onsite_kernel,
        out_shape=(struct((modes, modes), F32), struct((ROWS, TILE), F32)),
        in_specs=[INTO_SMEM] + [INTO_VMEM] * 3 + [ANY],
        out_specs=(INTO_VMEM,) * 2,
        compiler_params=PARAMS,
        cost_estimate=cost(8 * orbitals * modes * modes, 4 * orbitals * modes),
        name="onsite",
    )(place, w, factor, steps, yt)

    right, left = pl.pallas_call(
        couple_kernel,
        out_shape=(struct((modes, modes), F32),) * 2,
        in_specs=[INTO_VMEM] * 4 + [ANY],
        out_specs=(INTO_VMEM,) * 2,
        compiler_params=SMALL,
        cost_estimate=cost(4 * modes * modes * modes, 8 * modes * modes * 2),
        name="couple",
    )(yt, next_factor, factor, last_yt, done)
    return (onsite[None], right[None], left[None])


def solution(mesh):
    return jax.shard_map(
        shards,
        mesh=mesh,
        in_specs=(
            P(("groups", "slab"), None, None),
            P(("groups", "slab"), None, None, None),
            P(("groups", "slab"), None),
            P(("groups", "slab"), None),
            P(("groups", "slab"), None, None, None),
            P(("groups", "slab"), None),
            P(("groups", "slab"), None),
            P(("groups", "slab")),
        ),
        out_specs=(
            P(("groups", "slab"), None, None),
            P(("groups", "slab"), None, None),
            P(("groups", "slab"), None, None),
        ),
        check_vma=False,
    )
```

```python
import functools

import jax
import jax.numpy as jnp
from jax import lax
from jax.experimental import pallas as pl
from jax.experimental.pallas import tpu as pltpu
from jax.sharding import PartitionSpec as P

F32 = jnp.float32
BF16 = jnp.bfloat16
SURFACE = 4
TILE = 128
ROWS = 8


def lane(value, k):
    return jnp.broadcast_to(value[:, k : k + 1], value.shape)


def row(ref, k, width):
    return jnp.broadcast_to(ref[k : k + 1, :], (ROWS, width))


def three_parts(value):
    a = value.astype(BF16).astype(F32)
    b = (value - a).astype(BF16).astype(F32)
    return a, b, value - a - b


def exact_dot(a, b):
    a0, a1, a2 = (part.astype(BF16) for part in three_parts(a))
    b0, b1, b2 = (part.astype(BF16) for part in three_parts(b))
    return bf_dot(
        jnp.concatenate([a0, a0, a1, a1, a0, a2], axis=1),
        jnp.concatenate([b0, b1, b0, b1, b2, b0], axis=0),
        NN,
    )


def bf_dot(a, b, dims):
    return lax.dot_general(a, b, (dims, ((), ())), preferred_element_type=F32)


NN = ((1,), (0,))
TN = ((0,), (0,))
NT = ((1,), (1,))


def factor_tile(ax_ref, col_ref, below_ref, between):
    width = ax_ref.shape[1]
    panels = ax_ref.shape[0] // ROWS
    near = 2
    first_rows = ax_ref[:ROWS, :TILE]
    columns = [lane(first_rows, j) for j in range(ROWS)]
    for g in range(panels):
        base = ROWS * g
        for j in range(ROWS):
            col_ref[g % 2, j] = columns[j]
        s = {
            (i, j): row(col_ref.at[g % 2, j], i, TILE)
            for j in range(ROWS)
            for i in range(j, ROWS)
        }
        low, r = {}, []
        for p in range(0, ROWS, 2):
            q = p + 1
            a, b, c = s[p, p], s[q, p], s[q, q]
            root = lax.rsqrt(a * c - b * b)
            r_p = lax.rsqrt(a)
            r_q = a * r_p * root
            inverse = root * root
            r += [r_p, r_q]
            low[q, p] = b * r_p
            side = {}
            for i in range(q + 1, ROWS):
                first, second = s[i, p], s[i, q]
                low[i, p] = first * r_p
                low[i, q] = (second - low[i, p] * low[q, p]) * r_q
                side[i] = (c * first - b * second, a * second - b * first)
            for j in range(q + 1, ROWS):
                for i in range(j, ROWS):
                    both = side[j][0] * s[i, p] + side[j][1] * s[i, q]
                    s[i, j] = s[i, j] - both * inverse
        blocks, belows = {}, {}
        for i in range(g + 1, min(g + 1 + near, panels)):
            block = ax_ref[ROWS * i : ROWS * (i + 1), :]
            below = []
            for k in range(ROWS):
                column = lane(block[:, :TILE], base + k)
                for m in range(k):
                    column = column - below[m] * low[k, m]
                below.append(column * r[k])
            blocks[i], belows[i] = block, below
        if g + 1 < panels:
            below = belows[g + 1]
            columns = [lane(blocks[g + 1][:, :TILE], base + ROWS + j) for j in range(ROWS)]
            for k in range(ROWS):
                below_ref[g % 2, k] = below[k]
                for j in range(ROWS):
                    columns[j] = columns[j] - below[k] * row(below_ref.at[g % 2, k], j, TILE)
        r2 = [jnp.concatenate([v, v], axis=1) for v in r]
        low2 = {key: jnp.concatenate([v, v], axis=1) for key, v in low.items()}
        z = []
        for k in range(ROWS):
            top = row(ax_ref, base + k, width)
            for m in range(k):
                top = top - low2[k, m] * z[m]
            z.append(top * r2[k])
        sub = lax.broadcasted_iota(jnp.int32, z[0].shape, 0)
        packed = z[0]
        for k in range(1, ROWS):
            packed = jnp.where(sub == k, z[k], packed)
        for i, block in blocks.items():
            for k in range(ROWS):
                block = block - jnp.concatenate([belows[i][k], belows[i][k]], axis=1) * z[k]
            ax_ref[ROWS * i : ROWS * (i + 1), :] = block
        ax_ref[base : base + ROWS, TILE:] = packed[:, TILE:]
        far = ROWS * (g + 1 + near)
        if far < ax_ref.shape[0]:
            a, b, c = three_parts(packed)
            left = jnp.concatenate([v[:, :TILE] for v in (a, a, b, b, a, c)], axis=0).astype(BF16)
            right = jnp.concatenate([a, b, a, b, c, a], axis=0).astype(BF16)
            product = bf_dot(left, right, TN)
            ax_ref[far:, :] = ax_ref[far:, :] - product[far:, :]
        between(g)


def add_product(j, live, acc_ref, source_ref, blocks_ref, rows_ref, cols_ref, row_base):
    to = pl.multiple_of((rows_ref[j] - row_base) * TILE, TILE)
    at = pl.multiple_of(cols_ref[j] * TILE, TILE)
    product = bf_dot(blocks_ref[j], source_ref[pl.ds(at, TILE), :], NN)
    if live is not None:
        product = jnp.where(live, product, 0.0)
    acc_ref[pl.ds(to, TILE), :] = acc_ref[pl.ds(to, TILE), :] + product


def factor_kernel(
    rows_ref,
    cols_ref,
    crows_ref,
    ccols_ref,
    next_hbm,
    u_hbm,
    blocks_hbm,
    cblocks_hbm,
    f_ref,
    packed_ref,
    yt_ref,
    w_ref,
    gram_ref,
    upper_ref,
    inv_ref,
    ax_ref,
    col_ref,
    below_ref,
    u_ref,
    turned_ref,
    blocks_ref,
    acc_ref,
    next_ref,
    cblocks_ref,
    hop_ref,
    m_ref,
    sems,
    u_sems,
):
    orbitals, modes = u_ref.shape
    surface = hop_ref.shape[0]
    tiles = modes // TILE
    panels = TILE // ROWS
    step = orbitals // panels
    chunks = u_sems.shape[0]
    long_step = orbitals // chunks
    copies = [
        pltpu.make_async_copy(
            u_hbm.at[pl.ds(c * long_step, long_step)],
            u_ref.at[pl.ds(c * long_step, long_step)],
            u_sems.at[c],
        )
        for c in range(chunks)
    ]
    more = [
        pltpu.make_async_copy(blocks_hbm, blocks_ref, sems.at[0]),
        pltpu.make_async_copy(cblocks_hbm, cblocks_ref, sems.at[1]),
        pltpu.make_async_copy(next_hbm, next_ref, sems.at[2]),
    ]
    for copy in copies + more:
        copy.start()
    acc_ref[...] = jnp.zeros_like(acc_ref)
    hop_ref[...] = jnp.zeros_like(hop_ref)
    inv_ref[...] = jnp.zeros_like(inv_ref)

    def tile_of(t):
        return slice(t * TILE, (t + 1) * TILE)

    def gram_part(lo, hi, first, size):
        piece = slice(first, first + size)
        turned = u_ref[piece, lo:hi].T
        turned_ref[lo:hi, piece] = turned
        product = bf_dot(turned, u_ref[piece, lo:], NN)
        if first == 0:
            gram_ref[lo:hi, lo:] = product
        else:
            gram_ref[lo:hi, lo:] = gram_ref[lo:hi, lo:] + product

    for c, copy in enumerate(copies):
        copy.wait()
        gram_part(0, TILE, c * long_step, long_step)

    def wait_more():
        for copy in more:
            copy.wait()

    def onsite_product(j):
        add_product(j, None, acc_ref, u_ref, blocks_ref, rows_ref, cols_ref, 0)

    def coupling_product(j):
        base = (orbitals - surface) // TILE
        add_product(j, None, hop_ref, next_ref, cblocks_ref, crows_ref, ccols_ref, base)

    def reduce_part(out_ref, base, source_ref, first):
        left = turned_ref[:, base + first : base + first + step]
        product = bf_dot(left, source_ref[first : first + step, :].astype(BF16), NN)
        out_ref[...] = product if first == 0 else out_ref[...] + product

    def schur(i, j, t):
        gram_ref[tile_of(i), tile_of(j)] = gram_ref[tile_of(i), tile_of(j)] - exact_dot(
            upper_ref[tile_of(t), tile_of(i)].T, upper_ref[tile_of(t), tile_of(j)]
        )

    def inverse_sum(i, t):
        width = slice(0, (t + 1) * TILE)
        inv_ref[tile_of(i), width] = inv_ref[tile_of(i), width] - exact_dot(
            upper_ref[tile_of(t), tile_of(i)].T, inv_ref[tile_of(t), width]
        )

    def inverse_row(i):
        width = slice(0, i * TILE)
        inv_ref[tile_of(i), width] = exact_dot(
            inv_ref[tile_of(i), tile_of(i)], inv_ref[tile_of(i), width]
        )

    call = functools.partial
    products = [call(onsite_product, j) for j in range(blocks_ref.shape[0])]
    products += [call(coupling_product, j) for j in range(cblocks_ref.shape[0])]
    reductions = [call(reduce_part, w_ref, 0, acc_ref, c * step) for c in range(panels)]
    reductions += [
        call(reduce_part, m_ref, orbitals - surface, hop_ref, first)
        for first in range(0, surface, step)
    ]
    plan = {(t, g): [] for t in range(tiles) for g in range(panels)}
    for g in range(panels):
        plan[0, g].append(call(gram_part, TILE, modes, g * step, step))
    plan[0, 3].append(wait_more)
    room = [(t, g) for t in range(tiles - 1) for g in range(panels)][4:]
    for n, work in enumerate(products):
        plan[room[n * len(room) // len(products)]].append(work)
    for n, work in enumerate(reductions):
        plan[tiles - 1, n * panels // len(reductions)].append(work)
    for t in range(1, tiles):
        late = []
        if t > 1:
            late.append(call(inverse_row, t - 1))
        late += [call(schur, i, j, t - 1) for i in range(t, tiles) for j in range(i, tiles)][1:]
        late += [call(inverse_sum, i, t - 1) for i in range(t, tiles)]
        for n, work in enumerate(late):
            plan[t, n * (panels - 2) // len(late)].insert(0, work)

    def one_tile(t):
        here = tile_of(t)
        tile = gram_ref[here, here]
        on_diagonal = lax.broadcasted_iota(jnp.int32, tile.shape, 0) == lax.broadcasted_iota(
            jnp.int32, tile.shape, 1
        )
        diagonal = jnp.where(on_diagonal, tile, 0.0)
        across = lax.rsqrt(jnp.sum(diagonal, axis=0, keepdims=True))
        down = lax.rsqrt(jnp.sum(diagonal, axis=1, keepdims=True))
        ax_ref[:, :TILE] = tile * across * down
        ax_ref[:, TILE:] = on_diagonal.astype(F32)

        def between(g):
            for work in plan[t, g]:
                work()

        factor_tile(ax_ref, col_ref, below_ref, between)
        x = ax_ref[:, TILE:] * across
        inv_ref[here, here] = x
        if t + 1 < tiles:
            upper_ref[here, (t + 1) * TILE :] = exact_dot(x, gram_ref[here, (t + 1) * TILE :])
            schur(t + 1, t + 1, t)
        else:
            inverse_row(t)

    def step_of(b, carry):
        for t in range(tiles):
            pl.when(b == t)(call(one_tile, t))
        return carry

    lax.fori_loop(0, tiles, step_of, 0)
    factor = inv_ref[...].T.astype(BF16)
    f_ref[...] = factor
    packed_ref[...] = factor[: 2 * TILE, :]
    packed_ref[TILE:, :TILE] = factor[2 * TILE :, 2 * TILE :]
    high, low = split(m_ref[...])
    yt_ref[...] = (bf_dot(high, factor, TN) + bf_dot(low, factor, TN)).astype(BF16)


def left_kernel(f_ref, last_yt_ref, left_ref):
    left_ref[...] = bf_dot(f_ref[...], last_yt_ref[...], TN)


def first_kernel(step_ref, u_hbm, head_hbm, steps_ref, sem):
    surface = head_hbm.shape[0]
    copy = pltpu.make_async_copy(u_hbm.at[pl.ds(0, surface)], head_hbm, sem.at[0])
    copy.start()
    steps_ref[...] = jnp.full(steps_ref.shape, step_ref[0], F32)
    copy.wait()


def split(value):
    high = value.astype(BF16)
    return high, (value - high.astype(F32)).astype(BF16)


def onsite_kernel(
    place_ref, w_ref, f_ref, steps_ref, yt_ref, next_ref, out_ref, right_ref, full_ref
):
    modes = f_ref.shape[0]
    w = w_ref[...]
    w = w + w.T
    f = f_ref[...]
    high, low = split(w)
    half = bf_dot(high, f, NN) + bf_dot(low, f, NN)
    high, low = split(half)
    full = bf_dot(f, high, TN) + bf_dot(f, low, TN)
    steps = steps_ref[...]
    reached = lax.broadcasted_iota(jnp.int32, steps.shape, 0) <= place_ref[0]
    potential = jnp.sum(jnp.where(reached, steps, 0.0), axis=0, keepdims=True)[:, :1]
    i = lax.broadcasted_iota(jnp.int32, (modes, modes), 0)
    j = lax.broadcasted_iota(jnp.int32, (modes, modes), 1)
    out_ref[...] = full + jnp.where(i == j, potential, 0.0)
    full_ref[...] = jnp.zeros_like(full_ref)
    full_ref[:TILE, :] = next_ref[:TILE, :]
    full_ref[TILE : 2 * TILE, TILE:] = next_ref[TILE:, TILE:]
    full_ref[2 * TILE :, 2 * TILE :] = next_ref[TILE:, :TILE]
    right_ref[...] = bf_dot(yt_ref[...], full_ref[...], TN)


def struct(shape, dtype):
    return jax.ShapeDtypeStruct(shape, dtype)


ANY = pl.BlockSpec(memory_space=pl.ANY)
INTO_VMEM = pl.BlockSpec(memory_space=pltpu.VMEM)
INTO_SMEM = pl.BlockSpec(memory_space=pltpu.SMEM)


def params(mebibytes):
    return pltpu.CompilerParams(vmem_limit_bytes=mebibytes * 1024 * 1024)


def passed_along(block, axis, distance):
    devices = range(lax.axis_size(axis))
    route = [(i - distance, i) for i in devices if i - distance in devices]
    return lax.ppermute(block, axis, route)


def cost(flops, moved):
    return pl.CostEstimate(flops=flops, bytes_accessed=moved, transcendentals=0)


def shards(
    trial_modes,
    onsite_blocks,
    onsite_rows,
    onsite_cols,
    coupling_blocks,
    coupling_rows,
    coupling_cols,
    potential_step,
):
    u = trial_modes[0]
    orbitals, modes = u.shape
    surface = SURFACE * TILE
    count = onsite_blocks.shape[1]
    links = coupling_blocks.shape[1]
    place = lax.axis_index("slab").astype(jnp.int32).reshape(1)
    slabs = lax.axis_size("slab")
    head, step_rows = pl.pallas_call(
        first_kernel,
        out_shape=(struct((surface, modes), BF16), struct((slabs, TILE), F32)),
        in_specs=[INTO_SMEM, ANY],
        out_specs=(ANY, INTO_VMEM),
        scratch_shapes=[pltpu.SemaphoreType.DMA((1,))],
        compiler_params=params(59),
        cost_estimate=cost(0, 4 * surface * modes),
        name="first",
    )(potential_step, u)
    next_head = passed_along(head, "slab", -1)
    steps = lax.all_to_all(step_rows, "slab", 0, 0, tiled=True)

    factor, packed, yt, w = pl.pallas_call(
        factor_kernel,
        out_shape=(
            struct((modes, modes), BF16),
            struct((modes - TILE, modes), BF16),
            struct((modes, modes), BF16),
            struct((modes, modes), F32),
        ),
        in_specs=[INTO_SMEM] * 4 + [ANY] * 4,
        out_specs=(INTO_VMEM,) * 4,
        scratch_shapes=[
            pltpu.VMEM((modes, modes), F32),
            pltpu.VMEM((modes, modes), F32),
            pltpu.VMEM((modes, modes), F32),
            pltpu.VMEM((TILE, 2 * TILE), F32),
            pltpu.VMEM((2, ROWS, ROWS, TILE), F32),
            pltpu.VMEM((2, ROWS, ROWS, TILE), F32),
            pltpu.VMEM((orbitals, modes), BF16),
            pltpu.VMEM((modes, orbitals), BF16),
            pltpu.VMEM((count, TILE, TILE), BF16),
            pltpu.VMEM((orbitals, modes), F32),
            pltpu.VMEM((surface, modes), BF16),
            pltpu.VMEM((links, TILE, TILE), BF16),
            pltpu.VMEM((surface, modes), F32),
            pltpu.VMEM((modes, modes), F32),
            pltpu.SemaphoreType.DMA((3,)),
            pltpu.SemaphoreType.DMA((8,)),
        ],
        compiler_params=params(59),
        cost_estimate=cost(8 * orbitals * modes * modes, orbitals * modes * 2),
        name="factor",
    )(
        onsite_rows[0],
        onsite_cols[0],
        coupling_rows[0],
        coupling_cols[0],
        next_head,
        u,
        onsite_blocks[0],
        coupling_blocks[0],
    )
    next_packed = passed_along(packed, "slab", -1)
    last_yt = passed_along(yt, "slab", 1)

    onsite, right = pl.pallas_call(
        onsite_kernel,
        out_shape=(struct((modes, modes), F32),) * 2,
        in_specs=[INTO_SMEM] + [INTO_VMEM] * 5,
        out_specs=(INTO_VMEM,) * 2,
        scratch_shapes=[pltpu.VMEM((modes, modes), BF16)],
        compiler_params=params(16),
        cost_estimate=cost(8 * orbitals * modes * modes, 4 * orbitals * modes),
        name="onsite",
    )(place, w, factor, steps, yt, next_packed)

    left = pl.pallas_call(
        left_kernel,
        out_shape=struct((modes, modes), F32),
        in_specs=[INTO_VMEM] * 2,
        out_specs=INTO_VMEM,
        compiler_params=params(8),
        cost_estimate=cost(2 * modes * modes * modes, 8 * modes * modes),
        name="left",
    )(factor, last_yt)
    return (onsite[None], right[None], left[None])


def solution(mesh):
    return jax.shard_map(
        shards,
        mesh=mesh,
        in_specs=(
            P(("groups", "slab"), None, None),
            P(("groups", "slab"), None, None, None),
            P(("groups", "slab"), None),
            P(("groups", "slab"), None),
            P(("groups", "slab"), None, None, None),
            P(("groups", "slab"), None),
            P(("groups", "slab"), None),
            P(("groups", "slab")),
        ),
        out_specs=(
            P(("groups", "slab"), None, None),
            P(("groups", "slab"), None, None),
            P(("groups", "slab"), None, None),
        ),
        check_vma=False,
    )
```

```python
import functools

import jax
import jax.numpy as jnp
from jax import lax
from jax.experimental import pallas as pl
from jax.experimental.pallas import tpu as pltpu
from jax.sharding import PartitionSpec as P

F32 = jnp.float32
BF16 = jnp.bfloat16
SURFACE = 4
TILE = 128
ROWS = 8


def lane(value, k):
    return jnp.broadcast_to(value[:, k : k + 1], value.shape)


def row(ref, k, width):
    return jnp.broadcast_to(ref[k : k + 1, :], (ROWS, width))


def three_parts(value):
    a = value.astype(BF16).astype(F32)
    b = (value - a).astype(BF16).astype(F32)
    return a, b, value - a - b


def exact_dot(a, b):
    a0, a1, a2 = (part.astype(BF16) for part in three_parts(a))
    b0, b1, b2 = (part.astype(BF16) for part in three_parts(b))
    return bf_dot(
        jnp.concatenate([a0, a0, a1, a1, a0, a2], axis=1),
        jnp.concatenate([b0, b1, b0, b1, b2, b0], axis=0),
        NN,
    )


def bf_dot(a, b, dims):
    return lax.dot_general(a, b, (dims, ((), ())), preferred_element_type=F32)


NN = ((1,), (0,))
TN = ((0,), (0,))
NT = ((1,), (1,))


def factor_tile(ax_ref, col_ref, below_ref, between):
    width = ax_ref.shape[1]
    panels = ax_ref.shape[0] // ROWS
    near = 2
    first_rows = ax_ref[:ROWS, :TILE]
    columns = [lane(first_rows, j) for j in range(ROWS)]
    for g in range(panels):
        base = ROWS * g
        for j in range(ROWS):
            col_ref[g % 2, j] = columns[j]
        s = {
            (i, j): row(col_ref.at[g % 2, j], i, TILE)
            for j in range(ROWS)
            for i in range(j, ROWS)
        }
        low, r = {}, []
        for p in range(0, ROWS, 2):
            q = p + 1
            a, b, c = s[p, p], s[q, p], s[q, q]
            root = lax.rsqrt(a * c - b * b)
            r_p = lax.rsqrt(a)
            r_q = a * r_p * root
            inverse = root * root
            r += [r_p, r_q]
            low[q, p] = b * r_p
            side = {}
            for i in range(q + 1, ROWS):
                first, second = s[i, p], s[i, q]
                low[i, p] = first * r_p
                low[i, q] = (second - low[i, p] * low[q, p]) * r_q
                side[i] = (c * first - b * second, a * second - b * first)
            for j in range(q + 1, ROWS):
                for i in range(j, ROWS):
                    both = side[j][0] * s[i, p] + side[j][1] * s[i, q]
                    s[i, j] = s[i, j] - both * inverse
        blocks, belows = {}, {}
        for i in range(g + 1, min(g + 1 + near, panels)):
            block = ax_ref[ROWS * i : ROWS * (i + 1), :]
            below = []
            for k in range(ROWS):
                column = lane(block[:, :TILE], base + k)
                for m in range(k):
                    column = column - below[m] * low[k, m]
                below.append(column * r[k])
            blocks[i], belows[i] = block, below
        if g + 1 < panels:
            below = belows[g + 1]
            columns = [lane(blocks[g + 1][:, :TILE], base + ROWS + j) for j in range(ROWS)]
            for k in range(ROWS):
                below_ref[g % 2, k] = below[k]
                for j in range(ROWS):
                    columns[j] = columns[j] - below[k] * row(below_ref.at[g % 2, k], j, TILE)
        r2 = [jnp.concatenate([v, v], axis=1) for v in r]
        low2 = {key: jnp.concatenate([v, v], axis=1) for key, v in low.items()}
        z = []
        for k in range(ROWS):
            top = row(ax_ref, base + k, width)
            for m in range(k):
                top = top - low2[k, m] * z[m]
            z.append(top * r2[k])
        sub = lax.broadcasted_iota(jnp.int32, z[0].shape, 0)
        packed = z[0]
        for k in range(1, ROWS):
            packed = jnp.where(sub == k, z[k], packed)
        for i, block in blocks.items():
            for k in range(ROWS):
                block = block - jnp.concatenate([belows[i][k], belows[i][k]], axis=1) * z[k]
            ax_ref[ROWS * i : ROWS * (i + 1), :] = block
        ax_ref[base : base + ROWS, TILE:] = packed[:, TILE:]
        far = ROWS * (g + 1 + near)
        if far < ax_ref.shape[0]:
            a, b, c = three_parts(packed)
            left = jnp.concatenate([v[:, :TILE] for v in (a, a, b, b, a, c)], axis=0).astype(BF16)
            right = jnp.concatenate([a, b, a, b, c, a], axis=0).astype(BF16)
            product = bf_dot(left, right, TN)
            ax_ref[far:, :] = ax_ref[far:, :] - product[far:, :]
        between(g)


def add_product(j, live, acc_ref, source_ref, blocks_ref, rows_ref, cols_ref, row_base):
    to = pl.multiple_of((rows_ref[j] - row_base) * TILE, TILE)
    at = pl.multiple_of(cols_ref[j] * TILE, TILE)
    product = bf_dot(blocks_ref[j], source_ref[pl.ds(at, TILE), :], NN)
    if live is not None:
        product = jnp.where(live, product, 0.0)
    acc_ref[pl.ds(to, TILE), :] = acc_ref[pl.ds(to, TILE), :] + product


def factor_kernel(
    rows_ref,
    cols_ref,
    crows_ref,
    ccols_ref,
    next_hbm,
    u_hbm,
    blocks_hbm,
    cblocks_hbm,
    f_ref,
    packed_ref,
    yt_ref,
    w_ref,
    gram_ref,
    upper_ref,
    inv_ref,
    ax_ref,
    col_ref,
    below_ref,
    u_ref,
    turned_ref,
    blocks_ref,
    acc_ref,
    next_ref,
    cblocks_ref,
    hop_ref,
    m_ref,
    sems,
    u_sems,
):
    orbitals, modes = u_ref.shape
    surface = hop_ref.shape[0]
    tiles = modes // TILE
    panels = TILE // ROWS
    step = orbitals // panels
    chunks = u_sems.shape[0]
    long_step = orbitals // chunks
    copies = [
        pltpu.make_async_copy(
            u_hbm.at[pl.ds(c * long_step, long_step)],
            u_ref.at[pl.ds(c * long_step, long_step)],
            u_sems.at[c],
        )
        for c in range(chunks)
    ]
    more = [
        pltpu.make_async_copy(blocks_hbm, blocks_ref, sems.at[0]),
        pltpu.make_async_copy(cblocks_hbm, cblocks_ref, sems.at[1]),
        pltpu.make_async_copy(next_hbm, next_ref, sems.at[2]),
    ]
    for copy in copies + more:
        copy.start()
    acc_ref[...] = jnp.zeros_like(acc_ref)
    hop_ref[...] = jnp.zeros_like(hop_ref)
    inv_ref[...] = jnp.zeros_like(inv_ref)

    def tile_of(t):
        return slice(t * TILE, (t + 1) * TILE)

    def gram_part(lo, hi, first, size):
        piece = slice(first, first + size)
        turned = u_ref[piece, lo:hi].T
        turned_ref[lo:hi, piece] = turned
        product = bf_dot(turned, u_ref[piece, lo:], NN)
        if first == 0:
            gram_ref[lo:hi, lo:] = product
        else:
            gram_ref[lo:hi, lo:] = gram_ref[lo:hi, lo:] + product

    for c, copy in enumerate(copies):
        copy.wait()
        gram_part(0, TILE, c * long_step, long_step)

    def wait_more():
        for copy in more:
            copy.wait()

    def onsite_product(j):
        add_product(j, None, acc_ref, u_ref, blocks_ref, rows_ref, cols_ref, 0)

    def coupling_product(j):
        base = (orbitals - surface) // TILE
        add_product(j, None, hop_ref, next_ref, cblocks_ref, crows_ref, ccols_ref, base)

    def reduce_part(out_ref, base, source_ref, first):
        left = turned_ref[:, base + first : base + first + step]
        product = bf_dot(left, source_ref[first : first + step, :].astype(BF16), NN)
        out_ref[...] = product if first == 0 else out_ref[...] + product

    def schur(i, j, t):
        gram_ref[tile_of(i), tile_of(j)] = gram_ref[tile_of(i), tile_of(j)] - exact_dot(
            upper_ref[tile_of(t), tile_of(i)].T, upper_ref[tile_of(t), tile_of(j)]
        )

    def inverse_sum(i, t):
        width = slice(0, (t + 1) * TILE)
        inv_ref[tile_of(i), width] = inv_ref[tile_of(i), width] - exact_dot(
            upper_ref[tile_of(t), tile_of(i)].T, inv_ref[tile_of(t), width]
        )

    def inverse_row(i):
        width = slice(0, i * TILE)
        inv_ref[tile_of(i), width] = exact_dot(
            inv_ref[tile_of(i), tile_of(i)], inv_ref[tile_of(i), width]
        )

    call = functools.partial
    products = [call(onsite_product, j) for j in range(blocks_ref.shape[0])]
    products += [call(coupling_product, j) for j in range(cblocks_ref.shape[0])]
    reductions = [call(reduce_part, w_ref, 0, acc_ref, c * step) for c in range(panels)]
    reductions += [
        call(reduce_part, m_ref, orbitals - surface, hop_ref, first)
        for first in range(0, surface, step)
    ]
    plan = {(t, g): [] for t in range(tiles) for g in range(panels)}
    for g in range(panels):
        plan[0, g].append(call(gram_part, TILE, modes, g * step, step))
    plan[0, 3].append(wait_more)
    room = [(t, g) for t in range(tiles - 1) for g in range(panels)][4:]
    for n, work in enumerate(products):
        plan[room[n * len(room) // len(products)]].append(work)
    for n, work in enumerate(reductions):
        plan[tiles - 1, n * panels // len(reductions)].append(work)
    for t in range(1, tiles):
        late = []
        if t > 1:
            late.append(call(inverse_row, t - 1))
        late += [call(schur, i, j, t - 1) for i in range(t, tiles) for j in range(i, tiles)][1:]
        late += [call(inverse_sum, i, t - 1) for i in range(t, tiles)]
        for n, work in enumerate(late):
            plan[t, n * (panels - 2) // len(late)].insert(0, work)

    def one_tile(t):
        here = tile_of(t)
        tile = gram_ref[here, here]
        on_diagonal = lax.broadcasted_iota(jnp.int32, tile.shape, 0) == lax.broadcasted_iota(
            jnp.int32, tile.shape, 1
        )
        diagonal = jnp.where(on_diagonal, tile, 0.0)
        across = lax.rsqrt(jnp.sum(diagonal, axis=0, keepdims=True))
        down = lax.rsqrt(jnp.sum(diagonal, axis=1, keepdims=True))
        ax_ref[:, :TILE] = tile * across * down
        ax_ref[:, TILE:] = on_diagonal.astype(F32)

        def between(g):
            for work in plan[t, g]:
                work()

        factor_tile(ax_ref, col_ref, below_ref, between)
        x = ax_ref[:, TILE:] * across
        inv_ref[here, here] = x
        if t + 1 < tiles:
            upper_ref[here, (t + 1) * TILE :] = exact_dot(x, gram_ref[here, (t + 1) * TILE :])
            schur(t + 1, t + 1, t)
        else:
            inverse_row(t)

    def step_of(b, carry):
        for t in range(tiles):
            pl.when(b == t)(call(one_tile, t))
        return carry

    lax.fori_loop(0, tiles, step_of, 0)
    factor = inv_ref[...].T.astype(BF16)
    f_ref[...] = factor
    packed_ref[...] = factor[: 2 * TILE, :]
    packed_ref[TILE:, :TILE] = factor[2 * TILE :, 2 * TILE :]
    high, low = split(m_ref[...])
    yt_ref[...] = (bf_dot(high, factor, TN) + bf_dot(low, factor, TN)).astype(BF16)


def couple_kernel(yt_ref, next_ref, f_ref, last_yt_ref, right_ref, left_ref, full_ref):
    full_ref[...] = jnp.zeros_like(full_ref)
    full_ref[:TILE, :] = next_ref[:TILE, :]
    full_ref[TILE : 2 * TILE, TILE:] = next_ref[TILE:, TILE:]
    full_ref[2 * TILE :, 2 * TILE :] = next_ref[TILE:, :TILE]
    right_ref[...] = bf_dot(yt_ref[...], full_ref[...], TN)
    left_ref[...] = bf_dot(f_ref[...], last_yt_ref[...], TN)


def split(value):
    high = value.astype(BF16)
    return high, (value - high.astype(F32)).astype(BF16)


def onsite_kernel(place_ref, w_ref, f_ref, steps_ref, out_ref):
    modes = f_ref.shape[0]
    w = w_ref[...]
    w = w + w.T
    f = f_ref[...]
    high, low = split(w)
    half = bf_dot(high, f, NN) + bf_dot(low, f, NN)
    high, low = split(half)
    full = bf_dot(f, high, TN) + bf_dot(f, low, TN)
    steps = steps_ref[...]
    reached = lax.broadcasted_iota(jnp.int32, steps.shape, 0) <= place_ref[0]
    potential = jnp.sum(jnp.where(reached, steps, 0.0), axis=0, keepdims=True)[:, :1]
    i = lax.broadcasted_iota(jnp.int32, (modes, modes), 0)
    j = lax.broadcasted_iota(jnp.int32, (modes, modes), 1)
    out_ref[...] = full + jnp.where(i == j, potential, 0.0)


def struct(shape, dtype):
    return jax.ShapeDtypeStruct(shape, dtype)


ANY = pl.BlockSpec(memory_space=pl.ANY)
INTO_VMEM = pl.BlockSpec(memory_space=pltpu.VMEM)
INTO_SMEM = pl.BlockSpec(memory_space=pltpu.SMEM)


def params(mebibytes):
    return pltpu.CompilerParams(vmem_limit_bytes=mebibytes * 1024 * 1024)


def passed_along(block, axis, distance):
    devices = range(lax.axis_size(axis))
    route = [(i - distance, i) for i in devices if i - distance in devices]
    return lax.ppermute(block, axis, route)


def cost(flops, moved):
    return pl.CostEstimate(flops=flops, bytes_accessed=moved, transcendentals=0)


def shards(
    trial_modes,
    onsite_blocks,
    onsite_rows,
    onsite_cols,
    coupling_blocks,
    coupling_rows,
    coupling_cols,
    potential_step,
):
    u = trial_modes[0]
    orbitals, modes = u.shape
    surface = SURFACE * TILE
    count = onsite_blocks.shape[1]
    links = coupling_blocks.shape[1]
    place = lax.axis_index("slab").astype(jnp.int32).reshape(1)
    slabs = lax.axis_size("slab")
    next_head = passed_along(u[:surface], "slab", -1)
    steps = lax.all_to_all(
        jnp.broadcast_to(potential_step[:, None], (slabs, TILE)), "slab", 0, 0, tiled=True
    )

    factor, packed, yt, w = pl.pallas_call(
        factor_kernel,
        out_shape=(
            struct((modes, modes), BF16),
            struct((modes - TILE, modes), BF16),
            struct((modes, modes), BF16),
            struct((modes, modes), F32),
        ),
        in_specs=[INTO_SMEM] * 4 + [ANY] * 4,
        out_specs=(INTO_VMEM,) * 4,
        scratch_shapes=[
            pltpu.VMEM((modes, modes), F32),
            pltpu.VMEM((modes, modes), F32),
            pltpu.VMEM((modes, modes), F32),
            pltpu.VMEM((TILE, 2 * TILE), F32),
            pltpu.VMEM((2, ROWS, ROWS, TILE), F32),
            pltpu.VMEM((2, ROWS, ROWS, TILE), F32),
            pltpu.VMEM((orbitals, modes), BF16),
            pltpu.VMEM((modes, orbitals), BF16),
            pltpu.VMEM((count, TILE, TILE), BF16),
            pltpu.VMEM((orbitals, modes), F32),
            pltpu.VMEM((surface, modes), BF16),
            pltpu.VMEM((links, TILE, TILE), BF16),
            pltpu.VMEM((surface, modes), F32),
            pltpu.VMEM((modes, modes), F32),
            pltpu.SemaphoreType.DMA((3,)),
            pltpu.SemaphoreType.DMA((8,)),
        ],
        compiler_params=params(40),
        cost_estimate=cost(8 * orbitals * modes * modes, orbitals * modes * 2),
        name="factor",
    )(
        onsite_rows[0],
        onsite_cols[0],
        coupling_rows[0],
        coupling_cols[0],
        next_head,
        u,
        onsite_blocks[0],
        coupling_blocks[0],
    )
    next_packed = passed_along(packed, "slab", -1)
    last_yt = passed_along(yt, "slab", 1)

    onsite = pl.pallas_call(
        onsite_kernel,
        out_shape=struct((modes, modes), F32),
        in_specs=[INTO_SMEM] + [INTO_VMEM] * 3,
        out_specs=INTO_VMEM,
        compiler_params=params(40),
        cost_estimate=cost(8 * orbitals * modes * modes, 4 * orbitals * modes),
        name="onsite",
    )(place, w, factor, steps)

    right, left = pl.pallas_call(
        couple_kernel,
        out_shape=(struct((modes, modes), F32),) * 2,
        in_specs=[INTO_VMEM] * 4,
        out_specs=(INTO_VMEM,) * 2,
        scratch_shapes=[pltpu.VMEM((modes, modes), BF16)],
        compiler_params=params(40),
        cost_estimate=cost(4 * modes * modes * modes, 8 * modes * modes),
        name="couple",
    )(yt, next_packed, factor, last_yt)
    return (onsite[None], right[None], left[None])


def solution(mesh):
    return jax.shard_map(
        shards,
        mesh=mesh,
        in_specs=(
            P(("groups", "slab"), None, None),
            P(("groups", "slab"), None, None, None),
            P(("groups", "slab"), None),
            P(("groups", "slab"), None),
            P(("groups", "slab"), None, None, None),
            P(("groups", "slab"), None),
            P(("groups", "slab"), None),
            P(("groups", "slab")),
        ),
        out_specs=(
            P(("groups", "slab"), None, None),
            P(("groups", "slab"), None, None),
            P(("groups", "slab"), None, None),
        ),
        check_vma=False,
    )
```

```python
import functools

import jax
import jax.numpy as jnp
from jax import lax
from jax.experimental import pallas as pl
from jax.experimental.pallas import tpu as pltpu
from jax.sharding import PartitionSpec as P

F32 = jnp.float32
BF16 = jnp.bfloat16
SURFACE = 4
TILE = 128
ROWS = 8


def lane(value, k):
    return jnp.broadcast_to(value[:, k : k + 1], value.shape)


def row(ref, k, width):
    return jnp.broadcast_to(ref[k : k + 1, :], (ROWS, width))


def three_parts(value):
    a = value.astype(BF16).astype(F32)
    b = (value - a).astype(BF16).astype(F32)
    return a, b, value - a - b


def exact_dot(a, b):
    a0, a1, a2 = (part.astype(BF16) for part in three_parts(a))
    b0, b1, b2 = (part.astype(BF16) for part in three_parts(b))
    return bf_dot(
        jnp.concatenate([a0, a0, a1, a1, a0, a2], axis=1),
        jnp.concatenate([b0, b1, b0, b1, b2, b0], axis=0),
        NN,
    )


def bf_dot(a, b, dims):
    return lax.dot_general(a, b, (dims, ((), ())), preferred_element_type=F32)


NN = ((1,), (0,))
TN = ((0,), (0,))
NT = ((1,), (1,))


def factor_tile(ax_ref, col_ref, below_ref, between):
    width = ax_ref.shape[1]
    panels = ax_ref.shape[0] // ROWS
    near = 2
    first_rows = ax_ref[:ROWS, :TILE]
    columns = [lane(first_rows, j) for j in range(ROWS)]
    for g in range(panels):
        base = ROWS * g
        for j in range(ROWS):
            col_ref[g % 2, j] = columns[j]
        s = {
            (i, j): row(col_ref.at[g % 2, j], i, TILE)
            for j in range(ROWS)
            for i in range(j, ROWS)
        }
        low, r = {}, []
        for p in range(0, ROWS, 2):
            q = p + 1
            a, b, c = s[p, p], s[q, p], s[q, q]
            root = lax.rsqrt(a * c - b * b)
            r_p = lax.rsqrt(a)
            r_q = a * r_p * root
            inverse = root * root
            r += [r_p, r_q]
            low[q, p] = b * r_p
            side = {}
            for i in range(q + 1, ROWS):
                first, second = s[i, p], s[i, q]
                low[i, p] = first * r_p
                low[i, q] = (second - low[i, p] * low[q, p]) * r_q
                side[i] = (c * first - b * second, a * second - b * first)
            for j in range(q + 1, ROWS):
                for i in range(j, ROWS):
                    both = side[j][0] * s[i, p] + side[j][1] * s[i, q]
                    s[i, j] = s[i, j] - both * inverse
        blocks, belows = {}, {}
        for i in range(g + 1, min(g + 1 + near, panels)):
            block = ax_ref[ROWS * i : ROWS * (i + 1), :]
            below = []
            for k in range(ROWS):
                column = lane(block[:, :TILE], base + k)
                for m in range(k):
                    column = column - below[m] * low[k, m]
                below.append(column * r[k])
            blocks[i], belows[i] = block, below
        if g + 1 < panels:
            below = belows[g + 1]
            columns = [lane(blocks[g + 1][:, :TILE], base + ROWS + j) for j in range(ROWS)]
            for k in range(ROWS):
                below_ref[g % 2, k] = below[k]
                for j in range(ROWS):
                    columns[j] = columns[j] - below[k] * row(below_ref.at[g % 2, k], j, TILE)
        r2 = [jnp.concatenate([v, v], axis=1) for v in r]
        low2 = {key: jnp.concatenate([v, v], axis=1) for key, v in low.items()}
        z = []
        for k in range(ROWS):
            top = row(ax_ref, base + k, width)
            for m in range(k):
                top = top - low2[k, m] * z[m]
            z.append(top * r2[k])
        sub = lax.broadcasted_iota(jnp.int32, z[0].shape, 0)
        packed = z[0]
        for k in range(1, ROWS):
            packed = jnp.where(sub == k, z[k], packed)
        for i, block in blocks.items():
            for k in range(ROWS):
                block = block - jnp.concatenate([belows[i][k], belows[i][k]], axis=1) * z[k]
            ax_ref[ROWS * i : ROWS * (i + 1), :] = block
        ax_ref[base : base + ROWS, TILE:] = packed[:, TILE:]
        far = ROWS * (g + 1 + near)
        if far < ax_ref.shape[0]:
            a, b, c = three_parts(packed)
            left = jnp.concatenate([v[:, :TILE] for v in (a, a, b, b, a, c)], axis=0).astype(BF16)
            right = jnp.concatenate([a, b, a, b, c, a], axis=0).astype(BF16)
            product = bf_dot(left, right, TN)
            ax_ref[far:, :] = ax_ref[far:, :] - product[far:, :]
        between(g)


def add_product(j, live, acc_ref, source_ref, blocks_ref, rows_ref, cols_ref, row_base):
    to = pl.multiple_of((rows_ref[j] - row_base) * TILE, TILE)
    at = pl.multiple_of(cols_ref[j] * TILE, TILE)
    product = bf_dot(blocks_ref[j], source_ref[pl.ds(at, TILE), :], NN)
    if live is not None:
        product = jnp.where(live, product, 0.0)
    acc_ref[pl.ds(to, TILE), :] = acc_ref[pl.ds(to, TILE), :] + product


def factor_kernel(
    rows_ref,
    cols_ref,
    crows_ref,
    ccols_ref,
    next_hbm,
    u_hbm,
    blocks_hbm,
    cblocks_hbm,
    f_ref,
    packed_ref,
    yt_ref,
    turned_hbm,
    spread_hbm,
    gram_ref,
    upper_ref,
    inv_ref,
    ax_ref,
    col_ref,
    below_ref,
    u_ref,
    turned_ref,
    blocks_ref,
    acc_ref,
    spread_ref,
    next_ref,
    cblocks_ref,
    hop_ref,
    m_ref,
    sems,
    u_sems,
    out_sems,
):
    orbitals, modes = u_ref.shape
    surface = hop_ref.shape[0]
    tiles = modes // TILE
    panels = TILE // ROWS
    step = orbitals // panels
    chunks = u_sems.shape[0]
    long_step = orbitals // chunks
    copies = [
        pltpu.make_async_copy(
            u_hbm.at[pl.ds(c * long_step, long_step)],
            u_ref.at[pl.ds(c * long_step, long_step)],
            u_sems.at[c],
        )
        for c in range(chunks)
    ]
    more = [
        pltpu.make_async_copy(blocks_hbm, blocks_ref, sems.at[0]),
        pltpu.make_async_copy(cblocks_hbm, cblocks_ref, sems.at[1]),
        pltpu.make_async_copy(next_hbm, next_ref, sems.at[2]),
    ]
    for copy in copies + more:
        copy.start()
    acc_ref[...] = jnp.zeros_like(acc_ref)
    hop_ref[...] = jnp.zeros_like(hop_ref)
    inv_ref[...] = jnp.zeros_like(inv_ref)

    def tile_of(t):
        return slice(t * TILE, (t + 1) * TILE)

    def gram_part(lo, hi, first, size):
        piece = slice(first, first + size)
        turned = u_ref[piece, lo:hi].T
        turned_ref[lo:hi, piece] = turned
        product = bf_dot(turned, u_ref[piece, lo:], NN)
        if first == 0:
            gram_ref[lo:hi, lo:] = product
        else:
            gram_ref[lo:hi, lo:] = gram_ref[lo:hi, lo:] + product

    for c, copy in enumerate(copies):
        copy.wait()
        gram_part(0, TILE, c * long_step, long_step)

    def wait_more():
        for copy in more:
            copy.wait()

    def onsite_product(j):
        add_product(j, None, acc_ref, u_ref, blocks_ref, rows_ref, cols_ref, 0)

    def coupling_product(j):
        base = (orbitals - surface) // TILE
        add_product(j, None, hop_ref, next_ref, cblocks_ref, crows_ref, ccols_ref, base)

    def reduce_part(out_ref, base, source_ref, first):
        left = turned_ref[:, base + first : base + first + step]
        product = bf_dot(left, source_ref[first : first + step, :].astype(BF16), NN)
        out_ref[...] = product if first == 0 else out_ref[...] + product

    def schur(i, j, t):
        gram_ref[tile_of(i), tile_of(j)] = gram_ref[tile_of(i), tile_of(j)] - exact_dot(
            upper_ref[tile_of(t), tile_of(i)].T, upper_ref[tile_of(t), tile_of(j)]
        )

    def inverse_sum(i, t):
        width = slice(0, (t + 1) * TILE)
        inv_ref[tile_of(i), width] = inv_ref[tile_of(i), width] - exact_dot(
            upper_ref[tile_of(t), tile_of(i)].T, inv_ref[tile_of(t), width]
        )

    def inverse_row(i):
        width = slice(0, i * TILE)
        inv_ref[tile_of(i), width] = exact_dot(
            inv_ref[tile_of(i), tile_of(i)], inv_ref[tile_of(i), width]
        )

    outs = out_sems.shape[0] - 1
    out_step = orbitals // outs
    turned_copy = pltpu.make_async_copy(turned_ref, turned_hbm, out_sems.at[outs])
    spread_copies = [
        pltpu.make_async_copy(
            spread_ref.at[pl.ds(c * out_step, out_step)],
            spread_hbm.at[pl.ds(c * out_step, out_step)],
            out_sems.at[c],
        )
        for c in range(outs)
    ]

    def round_part(c):
        part = slice(c * out_step, (c + 1) * out_step)
        spread_ref[part, :] = acc_ref[part, :].astype(BF16)
        spread_copies[c].start()

    call = functools.partial
    products = [call(onsite_product, j) for j in range(blocks_ref.shape[0])]
    products += [call(coupling_product, j) for j in range(cblocks_ref.shape[0])]
    reductions = [
        call(reduce_part, m_ref, orbitals - surface, hop_ref, first)
        for first in range(0, surface, step)
    ]
    plan = {(t, g): [] for t in range(tiles) for g in range(panels)}
    for g in range(panels):
        plan[0, g].append(call(gram_part, TILE, modes, g * step, step))
    plan[0, 3].append(wait_more)
    room = [(t, g) for t in range(tiles - 1) for g in range(panels)][4:]
    for n, work in enumerate(products):
        plan[room[n * len(room) // len(products)]].append(work)
    plan[1, 0].append(turned_copy.start)
    for c in range(outs):
        plan[tiles - 1, c * (panels - 4) // outs].append(call(round_part, c))
    for n, work in enumerate(reductions):
        plan[tiles - 1, n * panels // len(reductions)].append(work)
    for t in range(1, tiles):
        late = []
        if t > 1:
            late.append(call(inverse_row, t - 1))
        late += [call(schur, i, j, t - 1) for i in range(t, tiles) for j in range(i, tiles)][1:]
        late += [call(inverse_sum, i, t - 1) for i in range(t, tiles)]
        for n, work in enumerate(late):
            plan[t, n * (panels - 2) // len(late)].insert(0, work)

    def one_tile(t):
        here = tile_of(t)
        tile = gram_ref[here, here]
        on_diagonal = lax.broadcasted_iota(jnp.int32, tile.shape, 0) == lax.broadcasted_iota(
            jnp.int32, tile.shape, 1
        )
        diagonal = jnp.where(on_diagonal, tile, 0.0)
        across = lax.rsqrt(jnp.sum(diagonal, axis=0, keepdims=True))
        down = lax.rsqrt(jnp.sum(diagonal, axis=1, keepdims=True))
        ax_ref[:, :TILE] = tile * across * down
        ax_ref[:, TILE:] = on_diagonal.astype(F32)

        def between(g):
            for work in plan[t, g]:
                work()

        factor_tile(ax_ref, col_ref, below_ref, between)
        x = ax_ref[:, TILE:] * across
        inv_ref[here, here] = x
        if t + 1 < tiles:
            upper_ref[here, (t + 1) * TILE :] = exact_dot(x, gram_ref[here, (t + 1) * TILE :])
            schur(t + 1, t + 1, t)
        else:
            inverse_row(t)

    def step_of(b, carry):
        for t in range(tiles):
            pl.when(b == t)(call(one_tile, t))
        return carry

    lax.fori_loop(0, tiles, step_of, 0)
    factor = inv_ref[...].T.astype(BF16)
    f_ref[...] = factor
    packed_ref[...] = factor[: 2 * TILE, :]
    packed_ref[TILE:, :TILE] = factor[2 * TILE :, 2 * TILE :]
    high, low = split(m_ref[...])
    yt_ref[...] = (bf_dot(high, factor, TN) + bf_dot(low, factor, TN)).astype(BF16)
    for copy in spread_copies + [turned_copy]:
        copy.wait()


def couple_kernel(yt_ref, next_ref, f_ref, last_yt_ref, right_ref, left_ref, full_ref):
    full_ref[...] = jnp.zeros_like(full_ref)
    full_ref[:TILE, :] = next_ref[:TILE, :]
    full_ref[TILE : 2 * TILE, TILE:] = next_ref[TILE:, TILE:]
    full_ref[2 * TILE :, 2 * TILE :] = next_ref[TILE:, :TILE]
    right_ref[...] = bf_dot(yt_ref[...], full_ref[...], TN)
    left_ref[...] = bf_dot(f_ref[...], last_yt_ref[...], TN)


def split(value):
    high = value.astype(BF16)
    return high, (value - high.astype(F32)).astype(BF16)


def onsite_kernel(
    place_ref, turned_hbm, spread_hbm, f_ref, steps_ref, out_ref, turned_ref, spread_ref, w_ref, sems
):
    modes = f_ref.shape[0]
    chunks = sems.shape[0]
    step = spread_ref.shape[0] // chunks
    copies = []
    for c in range(chunks):
        part = pl.ds(c * step, step)
        copies.append(
            [
                pltpu.make_async_copy(turned_hbm.at[:, part], turned_ref.at[:, part], sems.at[c, 0]),
                pltpu.make_async_copy(spread_hbm.at[part], spread_ref.at[part], sems.at[c, 1]),
            ]
        )
    for pair in copies:
        for copy in pair:
            copy.start()
    for c, pair in enumerate(copies):
        for copy in pair:
            copy.wait()
        part = slice(c * step, (c + 1) * step)
        product = bf_dot(turned_ref[:, part], spread_ref[part, :], NN)
        w_ref[...] = product if c == 0 else w_ref[...] + product
    w = w_ref[...]
    w = w + w.T
    f = f_ref[...]
    high, low = split(w)
    half = bf_dot(high, f, NN) + bf_dot(low, f, NN)
    high, low = split(half)
    full = bf_dot(f, high, TN) + bf_dot(f, low, TN)
    steps = steps_ref[...]
    reached = lax.broadcasted_iota(jnp.int32, steps.shape, 0) <= place_ref[0]
    potential = jnp.sum(jnp.where(reached, steps, 0.0), axis=0, keepdims=True)[:, :1]
    i = lax.broadcasted_iota(jnp.int32, (modes, modes), 0)
    j = lax.broadcasted_iota(jnp.int32, (modes, modes), 1)
    out_ref[...] = full + jnp.where(i == j, potential, 0.0)


def struct(shape, dtype):
    return jax.ShapeDtypeStruct(shape, dtype)


ANY = pl.BlockSpec(memory_space=pl.ANY)
INTO_VMEM = pl.BlockSpec(memory_space=pltpu.VMEM)
INTO_SMEM = pl.BlockSpec(memory_space=pltpu.SMEM)


def params(mebibytes):
    return pltpu.CompilerParams(vmem_limit_bytes=mebibytes * 1024 * 1024)


def passed_along(block, axis, distance):
    devices = range(lax.axis_size(axis))
    route = [(i - distance, i) for i in devices if i - distance in devices]
    return lax.ppermute(block, axis, route)


def cost(flops, moved):
    return pl.CostEstimate(flops=flops, bytes_accessed=moved, transcendentals=0)


def shards(
    trial_modes,
    onsite_blocks,
    onsite_rows,
    onsite_cols,
    coupling_blocks,
    coupling_rows,
    coupling_cols,
    potential_step,
):
    u = trial_modes[0]
    orbitals, modes = u.shape
    surface = SURFACE * TILE
    count = onsite_blocks.shape[1]
    links = coupling_blocks.shape[1]
    place = lax.axis_index("slab").astype(jnp.int32).reshape(1)
    slabs = lax.axis_size("slab")
    next_head = passed_along(u[:surface], "slab", -1)
    steps = lax.all_to_all(
        jnp.broadcast_to(potential_step[:, None], (slabs, TILE)), "slab", 0, 0, tiled=True
    )

    factor, packed, yt, turned, spread = pl.pallas_call(
        factor_kernel,
        out_shape=(
            struct((modes, modes), BF16),
            struct((modes - TILE, modes), BF16),
            struct((modes, modes), BF16),
            struct((modes, orbitals), BF16),
            struct((orbitals, modes), BF16),
        ),
        in_specs=[INTO_SMEM] * 4 + [ANY] * 4,
        out_specs=(INTO_VMEM,) * 3 + (ANY,) * 2,
        scratch_shapes=[
            pltpu.VMEM((modes, modes), F32),
            pltpu.VMEM((modes, modes), F32),
            pltpu.VMEM((modes, modes), F32),
            pltpu.VMEM((TILE, 2 * TILE), F32),
            pltpu.VMEM((2, ROWS, ROWS, TILE), F32),
            pltpu.VMEM((2, ROWS, ROWS, TILE), F32),
            pltpu.VMEM((orbitals, modes), BF16),
            pltpu.VMEM((modes, orbitals), BF16),
            pltpu.VMEM((count, TILE, TILE), BF16),
            pltpu.VMEM((orbitals, modes), F32),
            pltpu.VMEM((orbitals, modes), BF16),
            pltpu.VMEM((surface, modes), BF16),
            pltpu.VMEM((links, TILE, TILE), BF16),
            pltpu.VMEM((surface, modes), F32),
            pltpu.VMEM((modes, modes), F32),
            pltpu.SemaphoreType.DMA((3,)),
            pltpu.SemaphoreType.DMA((8,)),
            pltpu.SemaphoreType.DMA((5,)),
        ],
        compiler_params=params(59),
        cost_estimate=cost(8 * orbitals * modes * modes, orbitals * modes * 2),
        name="factor",
    )(
        onsite_rows[0],
        onsite_cols[0],
        coupling_rows[0],
        coupling_cols[0],
        next_head,
        u,
        onsite_blocks[0],
        coupling_blocks[0],
    )
    next_packed = passed_along(packed, "slab", -1)
    last_yt = passed_along(yt, "slab", 1)

    onsite = pl.pallas_call(
        onsite_kernel,
        out_shape=struct((modes, modes), F32),
        in_specs=[INTO_SMEM, ANY, ANY, INTO_VMEM, INTO_VMEM],
        out_specs=INTO_VMEM,
        scratch_shapes=[
            pltpu.VMEM((modes, orbitals), BF16),
            pltpu.VMEM((orbitals, modes), BF16),
            pltpu.VMEM((modes, modes), F32),
            pltpu.SemaphoreType.DMA((8, 2)),
        ],
        compiler_params=params(59),
        cost_estimate=cost(8 * orbitals * modes * modes, 4 * orbitals * modes),
        name="onsite",
    )(place, turned, spread, factor, steps)

    right, left = pl.pallas_call(
        couple_kernel,
        out_shape=(struct((modes, modes), F32),) * 2,
        in_specs=[INTO_VMEM] * 4,
        out_specs=(INTO_VMEM,) * 2,
        scratch_shapes=[pltpu.VMEM((modes, modes), BF16)],
        compiler_params=params(8),
        cost_estimate=cost(4 * modes * modes * modes, 8 * modes * modes),
        name="couple",
    )(yt, next_packed, factor, last_yt)
    return (onsite[None], right[None], left[None])


def solution(mesh):
    return jax.shard_map(
        shards,
        mesh=mesh,
        in_specs=(
            P(("groups", "slab"), None, None),
            P(("groups", "slab"), None, None, None),
            P(("groups", "slab"), None),
            P(("groups", "slab"), None),
            P(("groups", "slab"), None, None, None),
            P(("groups", "slab"), None),
            P(("groups", "slab"), None),
            P(("groups", "slab")),
        ),
        out_specs=(
            P(("groups", "slab"), None, None),
            P(("groups", "slab"), None, None),
            P(("groups", "slab"), None, None),
        ),
        check_vma=False,
    )
```

```python
import functools

import jax
import jax.numpy as jnp
from jax import lax
from jax.experimental import pallas as pl
from jax.experimental.pallas import tpu as pltpu
from jax.sharding import PartitionSpec as P

F32 = jnp.float32
BF16 = jnp.bfloat16
SURFACE = 4
TILE = 128
ROWS = 8


def lane(value, k):
    return jnp.broadcast_to(value[:, k : k + 1], value.shape)


def row(ref, k, width):
    return jnp.broadcast_to(ref[k : k + 1, :], (ROWS, width))


def three_parts(value):
    a = value.astype(BF16).astype(F32)
    b = (value - a).astype(BF16).astype(F32)
    return a, b, value - a - b


def exact_dot(a, b):
    a0, a1, a2 = (part.astype(BF16) for part in three_parts(a))
    b0, b1, b2 = (part.astype(BF16) for part in three_parts(b))
    return bf_dot(
        jnp.concatenate([a0, a0, a1, a1, a0, a2], axis=1),
        jnp.concatenate([b0, b1, b0, b1, b2, b0], axis=0),
        NN,
    )


def bf_dot(a, b, dims):
    return lax.dot_general(a, b, (dims, ((), ())), preferred_element_type=F32)


NN = ((1,), (0,))
TN = ((0,), (0,))
NT = ((1,), (1,))


def factor_tile(ax_ref, col_ref, below_ref, between):
    width = ax_ref.shape[1]
    panels = ax_ref.shape[0] // ROWS
    near = 2
    first_rows = ax_ref[:ROWS, :TILE]
    columns = [lane(first_rows, j) for j in range(ROWS)]
    for g in range(panels):
        base = ROWS * g
        for j in range(ROWS):
            col_ref[g % 2, j] = columns[j]
        s = {
            (i, j): row(col_ref.at[g % 2, j], i, TILE)
            for j in range(ROWS)
            for i in range(j, ROWS)
        }
        low, r = {}, []
        for p in range(0, ROWS, 2):
            q = p + 1
            a, b, c = s[p, p], s[q, p], s[q, q]
            root = lax.rsqrt(a * c - b * b)
            r_p = lax.rsqrt(a)
            r_q = a * r_p * root
            inverse = root * root
            r += [r_p, r_q]
            low[q, p] = b * r_p
            side = {}
            for i in range(q + 1, ROWS):
                first, second = s[i, p], s[i, q]
                low[i, p] = first * r_p
                low[i, q] = (second - low[i, p] * low[q, p]) * r_q
                side[i] = (c * first - b * second, a * second - b * first)
            for j in range(q + 1, ROWS):
                for i in range(j, ROWS):
                    both = side[j][0] * s[i, p] + side[j][1] * s[i, q]
                    s[i, j] = s[i, j] - both * inverse
        blocks, belows = {}, {}
        for i in range(g + 1, min(g + 1 + near, panels)):
            block = ax_ref[ROWS * i : ROWS * (i + 1), :]
            below = []
            for k in range(ROWS):
                column = lane(block[:, :TILE], base + k)
                for m in range(k):
                    column = column - below[m] * low[k, m]
                below.append(column * r[k])
            blocks[i], belows[i] = block, below
        if g + 1 < panels:
            below = belows[g + 1]
            columns = [lane(blocks[g + 1][:, :TILE], base + ROWS + j) for j in range(ROWS)]
            for k in range(ROWS):
                below_ref[g % 2, k] = below[k]
                for j in range(ROWS):
                    columns[j] = columns[j] - below[k] * row(below_ref.at[g % 2, k], j, TILE)
        r2 = [jnp.concatenate([v, v], axis=1) for v in r]
        low2 = {key: jnp.concatenate([v, v], axis=1) for key, v in low.items()}
        z = []
        for k in range(ROWS):
            top = row(ax_ref, base + k, width)
            for m in range(k):
                top = top - low2[k, m] * z[m]
            z.append(top * r2[k])
        sub = lax.broadcasted_iota(jnp.int32, z[0].shape, 0)
        packed = z[0]
        for k in range(1, ROWS):
            packed = jnp.where(sub == k, z[k], packed)
        for i, block in blocks.items():
            for k in range(ROWS):
                block = block - jnp.concatenate([belows[i][k], belows[i][k]], axis=1) * z[k]
            ax_ref[ROWS * i : ROWS * (i + 1), :] = block
        ax_ref[base : base + ROWS, TILE:] = packed[:, TILE:]
        far = ROWS * (g + 1 + near)
        if far < ax_ref.shape[0]:
            a, b, c = three_parts(packed)
            left = jnp.concatenate([v[:, :TILE] for v in (a, a, b, b, a, c)], axis=0).astype(BF16)
            right = jnp.concatenate([a, b, a, b, c, a], axis=0).astype(BF16)
            product = bf_dot(left, right, TN)
            ax_ref[far:, :] = ax_ref[far:, :] - product[far:, :]
        between(g)


def add_product(j, live, acc_ref, source_ref, blocks_ref, rows_ref, cols_ref, row_base):
    to = pl.multiple_of((rows_ref[j] - row_base) * TILE, TILE)
    at = pl.multiple_of(cols_ref[j] * TILE, TILE)
    product = bf_dot(blocks_ref[j], source_ref[pl.ds(at, TILE), :], NN)
    if live is not None:
        product = jnp.where(live, product, 0.0)
    acc_ref[pl.ds(to, TILE), :] = acc_ref[pl.ds(to, TILE), :] + product


def add_pair(t, table_ref, acc_ref, source_ref, blocks_ref):
    a, b = table_ref[0, 2 * t], table_ref[0, 2 * t + 1]
    to = pl.multiple_of(table_ref[1, 2 * t] * TILE, TILE)
    at_a = pl.multiple_of(table_ref[2, 2 * t] * TILE, TILE)
    at_b = pl.multiple_of(table_ref[2, 2 * t + 1] * TILE, TILE)
    left = jnp.concatenate([blocks_ref[a], blocks_ref[b]], axis=1)
    right = jnp.concatenate(
        [source_ref[pl.ds(at_a, TILE), :], source_ref[pl.ds(at_b, TILE), :]], axis=0
    )
    acc_ref[pl.ds(to, TILE), :] = acc_ref[pl.ds(to, TILE), :] + bf_dot(left, right, NN)


def pair_table(rows, cols, count):
    shape = (TILE, TILE)
    i = lax.broadcasted_iota(jnp.int32, shape, 0)
    j = lax.broadcasted_iota(jnp.int32, shape, 1)
    row_j, col_j = (jnp.broadcast_to(v.astype(F32), shape) for v in (rows, cols))
    row_i, col_i = row_j.T, col_j.T
    ones, none = jnp.ones(shape, F32), jnp.zeros(shape, F32)
    same = (row_i == row_j) & (i < count)
    rank_j = jnp.sum(jnp.where(same & (i < j), ones, none), axis=0, keepdims=True)
    size_j = jnp.sum(jnp.where(same, ones, none), axis=0, keepdims=True)
    half = jnp.floor(size_j * 0.5)
    odd_last = (size_j - 2.0 * half) * jnp.where(rank_j == size_j - 1.0, 1.0, 0.0)
    ahead = jnp.where(row_j < row_i, ones + odd_last, none)
    ahead = ahead + jnp.where((row_j == row_i) & (j < i), ones, none)
    place_i = jnp.sum(jnp.where(j < count, ahead, none), axis=1, keepdims=True)
    match = (place_i == j.astype(F32)) & (i < count)
    found = jnp.sum(jnp.where(match, ones, none), axis=0, keepdims=True)
    block = jnp.sum(jnp.where(match, i.astype(F32), none), axis=0, keepdims=True)
    block = block + (1.0 - found) * count
    row_of = jnp.sum(jnp.where(match, row_i, none), axis=0, keepdims=True)
    col_of = jnp.sum(jnp.where(match, col_i, none), axis=0, keepdims=True)
    return jnp.concatenate([block, row_of, col_of], axis=0).astype(jnp.int32)


def factor_kernel(
    crows_ref,
    ccols_ref,
    rows_ref,
    cols_ref,
    next_hbm,
    u_hbm,
    blocks_hbm,
    cblocks_hbm,
    f_ref,
    packed_ref,
    yt_ref,
    w_ref,
    gram_ref,
    upper_ref,
    inv_ref,
    ax_ref,
    col_ref,
    below_ref,
    u_ref,
    turned_ref,
    blocks_ref,
    acc_ref,
    next_ref,
    cblocks_ref,
    hop_ref,
    m_ref,
    index_ref,
    made_ref,
    table_ref,
    sems,
    u_sems,
):
    orbitals, modes = u_ref.shape
    surface = hop_ref.shape[0]
    count = blocks_hbm.shape[0]
    slots = (count + orbitals // TILE) // 2
    tiles = modes // TILE
    panels = TILE // ROWS
    step = orbitals // panels
    chunks = u_sems.shape[0]
    long_step = orbitals // chunks
    copies = [
        pltpu.make_async_copy(
            u_hbm.at[pl.ds(c * long_step, long_step)],
            u_ref.at[pl.ds(c * long_step, long_step)],
            u_sems.at[c],
        )
        for c in range(chunks)
    ]
    more = [
        pltpu.make_async_copy(blocks_hbm, blocks_ref.at[pl.ds(0, count)], sems.at[0]),
        pltpu.make_async_copy(cblocks_hbm, cblocks_ref, sems.at[1]),
        pltpu.make_async_copy(next_hbm, next_ref, sems.at[2]),
    ]
    for copy in copies + more:
        copy.start()
    index_ref[...] = jnp.zeros_like(index_ref)
    index_ref[0:1, :count] = rows_ref[...]
    index_ref[1:2, :count] = cols_ref[...]
    made_ref[0:3, :] = pair_table(index_ref[0:1, :], index_ref[1:2, :], count)
    more.append(pltpu.make_async_copy(made_ref, table_ref, sems.at[3]))
    more[-1].start()
    blocks_ref[count] = jnp.zeros_like(blocks_ref[count])
    acc_ref[...] = jnp.zeros_like(acc_ref)
    hop_ref[...] = jnp.zeros_like(hop_ref)
    inv_ref[...] = jnp.zeros_like(inv_ref)

    def tile_of(t):
        return slice(t * TILE, (t + 1) * TILE)

    def gram_part(lo, hi, first, size):
        piece = slice(first, first + size)
        turned = u_ref[piece, lo:hi].T
        turned_ref[lo:hi, piece] = turned
        product = bf_dot(turned, u_ref[piece, lo:], NN)
        if first == 0:
            gram_ref[lo:hi, lo:] = product
        else:
            gram_ref[lo:hi, lo:] = gram_ref[lo:hi, lo:] + product

    for c, copy in enumerate(copies):
        copy.wait()
        gram_part(0, TILE, c * long_step, long_step)

    def wait_more():
        for copy in more:
            copy.wait()

    def onsite_product(t):
        add_pair(t, table_ref, acc_ref, u_ref, blocks_ref)

    def coupling_product(j):
        base = (orbitals - surface) // TILE
        add_product(j, None, hop_ref, next_ref, cblocks_ref, crows_ref, ccols_ref, base)

    def reduce_part(out_ref, base, source_ref, first):
        left = turned_ref[:, base + first : base + first + step]
        product = bf_dot(left, source_ref[first : first + step, :].astype(BF16), NN)
        out_ref[...] = product if first == 0 else out_ref[...] + product

    def schur(i, j, t):
        gram_ref[tile_of(i), tile_of(j)] = gram_ref[tile_of(i), tile_of(j)] - exact_dot(
            upper_ref[tile_of(t), tile_of(i)].T, upper_ref[tile_of(t), tile_of(j)]
        )

    def inverse_sum(i, t):
        width = slice(0, (t + 1) * TILE)
        inv_ref[tile_of(i), width] = inv_ref[tile_of(i), width] - exact_dot(
            upper_ref[tile_of(t), tile_of(i)].T, inv_ref[tile_of(t), width]
        )

    def inverse_row(i):
        width = slice(0, i * TILE)
        inv_ref[tile_of(i), width] = exact_dot(
            inv_ref[tile_of(i), tile_of(i)], inv_ref[tile_of(i), width]
        )

    call = functools.partial
    products = [call(onsite_product, t) for t in range(slots)]
    links = [call(coupling_product, j) for j in range(cblocks_ref.shape[0])]
    reductions = [call(reduce_part, w_ref, 0, acc_ref, c * step) for c in range(panels)]
    finish = [
        call(reduce_part, m_ref, orbitals - surface, hop_ref, first)
        for first in range(0, surface, step)
    ]
    plan = {(t, g): [] for t in range(tiles) for g in range(panels)}
    for g in range(panels):
        plan[0, g].append(call(gram_part, TILE, modes, g * step, step))
    plan[0, 3].append(wait_more)
    room = [(0, g) for g in range(4, panels)]
    room += [(t, g) for t in range(1, tiles - 1) for g in range(panels) for _ in range(2)]
    for n, work in enumerate(products):
        plan[room[n * len(room) // len(products)]].append(work)
    for n, work in enumerate(reductions):
        plan[tiles - 1, n * panels // len(reductions)].append(work)
    for n, work in enumerate(links):
        plan[tiles - 1, n * (panels - 4) // len(links)].append(work)
    for n, work in enumerate(finish):
        plan[tiles - 1, panels - 3 + n].append(work)
    for t in range(1, tiles):
        late = []
        if t > 1:
            late.append(call(inverse_row, t - 1))
        late += [call(schur, i, j, t - 1) for i in range(t, tiles) for j in range(i, tiles)][1:]
        late += [call(inverse_sum, i, t - 1) for i in range(t, tiles)]
        for n, work in enumerate(late):
            plan[t, n * (panels - 2) // len(late)].insert(0, work)

    def one_tile(t):
        here = tile_of(t)
        tile = gram_ref[here, here]
        on_diagonal = lax.broadcasted_iota(jnp.int32, tile.shape, 0) == lax.broadcasted_iota(
            jnp.int32, tile.shape, 1
        )
        diagonal = jnp.where(on_diagonal, tile, 0.0)
        across = lax.rsqrt(jnp.sum(diagonal, axis=0, keepdims=True))
        down = lax.rsqrt(jnp.sum(diagonal, axis=1, keepdims=True))
        ax_ref[:, :TILE] = tile * across * down
        ax_ref[:, TILE:] = on_diagonal.astype(F32)

        def between(g):
            for work in plan[t, g]:
                work()

        factor_tile(ax_ref, col_ref, below_ref, between)
        x = ax_ref[:, TILE:] * across
        inv_ref[here, here] = x
        if t + 1 < tiles:
            upper_ref[here, (t + 1) * TILE :] = exact_dot(x, gram_ref[here, (t + 1) * TILE :])
            schur(t + 1, t + 1, t)
        else:
            inverse_row(t)

    def step_of(b, carry):
        for t in range(tiles):
            pl.when(b == t)(call(one_tile, t))
        return carry

    lax.fori_loop(0, tiles, step_of, 0)
    factor = inv_ref[...].T.astype(BF16)
    f_ref[...] = factor
    packed_ref[...] = factor[: 2 * TILE, :]
    packed_ref[TILE:, :TILE] = factor[2 * TILE :, 2 * TILE :]
    high, low = split(m_ref[...])
    yt_ref[...] = (bf_dot(high, factor, TN) + bf_dot(low, factor, TN)).astype(BF16)


def couple_kernel(yt_ref, next_ref, f_ref, last_yt_ref, right_ref, left_ref, full_ref):
    full_ref[...] = jnp.zeros_like(full_ref)
    full_ref[:TILE, :] = next_ref[:TILE, :]
    full_ref[TILE : 2 * TILE, TILE:] = next_ref[TILE:, TILE:]
    full_ref[2 * TILE :, 2 * TILE :] = next_ref[TILE:, :TILE]
    right_ref[...] = bf_dot(yt_ref[...], full_ref[...], TN)
    left_ref[...] = bf_dot(f_ref[...], last_yt_ref[...], TN)


def split(value):
    high = value.astype(BF16)
    return high, (value - high.astype(F32)).astype(BF16)


def onsite_kernel(place_ref, w_ref, f_ref, steps_ref, out_ref):
    modes = f_ref.shape[0]
    w = w_ref[...]
    w = w + w.T
    f = f_ref[...]
    high, low = split(w)
    half = bf_dot(high, f, NN) + bf_dot(low, f, NN)
    high, low = split(half)
    full = bf_dot(f, high, TN) + bf_dot(f, low, TN)
    steps = steps_ref[...]
    reached = lax.broadcasted_iota(jnp.int32, steps.shape, 0) <= place_ref[0]
    potential = jnp.sum(jnp.where(reached, steps, 0.0), axis=0, keepdims=True)[:, :1]
    i = lax.broadcasted_iota(jnp.int32, (modes, modes), 0)
    j = lax.broadcasted_iota(jnp.int32, (modes, modes), 1)
    out_ref[...] = full + jnp.where(i == j, potential, 0.0)


def struct(shape, dtype):
    return jax.ShapeDtypeStruct(shape, dtype)


ANY = pl.BlockSpec(memory_space=pl.ANY)
INTO_VMEM = pl.BlockSpec(memory_space=pltpu.VMEM)
INTO_SMEM = pl.BlockSpec(memory_space=pltpu.SMEM)


def params(mebibytes):
    return pltpu.CompilerParams(vmem_limit_bytes=mebibytes * 1024 * 1024)


def passed_along(block, axis, distance):
    devices = range(lax.axis_size(axis))
    route = [(i - distance, i) for i in devices if i - distance in devices]
    return lax.ppermute(block, axis, route)


def cost(flops, moved):
    return pl.CostEstimate(flops=flops, bytes_accessed=moved, transcendentals=0)


def shards(
    trial_modes,
    onsite_blocks,
    onsite_rows,
    onsite_cols,
    coupling_blocks,
    coupling_rows,
    coupling_cols,
    potential_step,
):
    u = trial_modes[0]
    orbitals, modes = u.shape
    surface = SURFACE * TILE
    count = onsite_blocks.shape[1]
    links = coupling_blocks.shape[1]
    place = lax.axis_index("slab").astype(jnp.int32).reshape(1)
    slabs = lax.axis_size("slab")
    next_head = passed_along(u[:surface], "slab", -1)
    steps = lax.all_to_all(
        jnp.broadcast_to(potential_step[:, None], (slabs, TILE)), "slab", 0, 0, tiled=True
    )

    factor, packed, yt, w = pl.pallas_call(
        factor_kernel,
        out_shape=(
            struct((modes, modes), BF16),
            struct((modes - TILE, modes), BF16),
            struct((modes, modes), BF16),
            struct((modes, modes), F32),
        ),
        in_specs=[INTO_SMEM] * 2 + [INTO_VMEM] * 2 + [ANY] * 4,
        out_specs=(INTO_VMEM,) * 4,
        scratch_shapes=[
            pltpu.VMEM((modes, modes), F32),
            pltpu.VMEM((modes, modes), F32),
            pltpu.VMEM((modes, modes), F32),
            pltpu.VMEM((TILE, 2 * TILE), F32),
            pltpu.VMEM((2, ROWS, ROWS, TILE), F32),
            pltpu.VMEM((2, ROWS, ROWS, TILE), F32),
            pltpu.VMEM((orbitals, modes), BF16),
            pltpu.VMEM((modes, orbitals), BF16),
            pltpu.VMEM((count + 1, TILE, TILE), BF16),
            pltpu.VMEM((orbitals, modes), F32),
            pltpu.VMEM((surface, modes), BF16),
            pltpu.VMEM((links, TILE, TILE), BF16),
            pltpu.VMEM((surface, modes), F32),
            pltpu.VMEM((modes, modes), F32),
            pltpu.VMEM((ROWS, TILE), jnp.int32),
            pltpu.VMEM((ROWS, TILE), jnp.int32),
            pltpu.SMEM((ROWS, TILE), jnp.int32),
            pltpu.SemaphoreType.DMA((4,)),
            pltpu.SemaphoreType.DMA((8,)),
        ],
        compiler_params=params(59),
        cost_estimate=cost(8 * orbitals * modes * modes, orbitals * modes * 2),
        name="factor",
    )(
        coupling_rows[0],
        coupling_cols[0],
        onsite_rows,
        onsite_cols,
        next_head,
        u,
        onsite_blocks[0],
        coupling_blocks[0],
    )
    next_packed = passed_along(packed, "slab", -1)
    last_yt = passed_along(yt, "slab", 1)

    onsite = pl.pallas_call(
        onsite_kernel,
        out_shape=struct((modes, modes), F32),
        in_specs=[INTO_SMEM] + [INTO_VMEM] * 3,
        out_specs=INTO_VMEM,
        compiler_params=params(60),
        cost_estimate=cost(8 * orbitals * modes * modes, 4 * orbitals * modes),
        name="onsite",
    )(place, w, factor, steps)

    right, left = pl.pallas_call(
        couple_kernel,
        out_shape=(struct((modes, modes), F32),) * 2,
        in_specs=[INTO_VMEM] * 4,
        out_specs=(INTO_VMEM,) * 2,
        scratch_shapes=[pltpu.VMEM((modes, modes), BF16)],
        compiler_params=params(8),
        cost_estimate=cost(4 * modes * modes * modes, 8 * modes * modes),
        name="couple",
    )(yt, next_packed, factor, last_yt)
    return (onsite[None], right[None], left[None])


def solution(mesh):
    return jax.shard_map(
        shards,
        mesh=mesh,
        in_specs=(
            P(("groups", "slab"), None, None),
            P(("groups", "slab"), None, None, None),
            P(("groups", "slab"), None),
            P(("groups", "slab"), None),
            P(("groups", "slab"), None, None, None),
            P(("groups", "slab"), None),
            P(("groups", "slab"), None),
            P(("groups", "slab")),
        ),
        out_specs=(
            P(("groups", "slab"), None, None),
            P(("groups", "slab"), None, None),
            P(("groups", "slab"), None, None),
        ),
        check_vma=False,
    )
```

```python
import functools

import jax
import jax.numpy as jnp
from jax import lax
from jax.experimental import pallas as pl
from jax.experimental.pallas import tpu as pltpu
from jax.sharding import PartitionSpec as P

F32 = jnp.float32
BF16 = jnp.bfloat16
SURFACE = 4
TILE = 128
ROWS = 8


def lane(value, k):
    return jnp.broadcast_to(value[:, k : k + 1], value.shape)


def row(ref, k, width):
    return jnp.broadcast_to(ref[k : k + 1, :], (ROWS, width))


def three_parts(value):
    a = value.astype(BF16).astype(F32)
    b = (value - a).astype(BF16).astype(F32)
    return a, b, value - a - b


def exact_dot(a, b):
    a0, a1, a2 = (part.astype(BF16) for part in three_parts(a))
    b0, b1, b2 = (part.astype(BF16) for part in three_parts(b))
    return bf_dot(
        jnp.concatenate([a0, a0, a1, a1, a0, a2], axis=1),
        jnp.concatenate([b0, b1, b0, b1, b2, b0], axis=0),
        NN,
    )


def bf_dot(a, b, dims):
    return lax.dot_general(a, b, (dims, ((), ())), preferred_element_type=F32)


NN = ((1,), (0,))
TN = ((0,), (0,))
NT = ((1,), (1,))


def factor_tile(ax_ref, col_ref, below_ref, between):
    width = ax_ref.shape[1]
    panels = ax_ref.shape[0] // ROWS
    near = 2
    first_rows = ax_ref[:ROWS, :TILE]
    columns = [lane(first_rows, j) for j in range(ROWS)]
    for g in range(panels):
        base = ROWS * g
        for j in range(ROWS):
            col_ref[g % 2, j] = columns[j]
        s = {
            (i, j): row(col_ref.at[g % 2, j], i, TILE)
            for j in range(ROWS)
            for i in range(j, ROWS)
        }
        low, r = {}, []
        for p in range(0, ROWS, 2):
            q = p + 1
            a, b, c = s[p, p], s[q, p], s[q, q]
            root = lax.rsqrt(a * c - b * b)
            r_p = lax.rsqrt(a)
            r_q = a * r_p * root
            inverse = root * root
            r += [r_p, r_q]
            low[q, p] = b * r_p
            side = {}
            for i in range(q + 1, ROWS):
                first, second = s[i, p], s[i, q]
                low[i, p] = first * r_p
                low[i, q] = (second - low[i, p] * low[q, p]) * r_q
                side[i] = (c * first - b * second, a * second - b * first)
            for j in range(q + 1, ROWS):
                for i in range(j, ROWS):
                    both = side[j][0] * s[i, p] + side[j][1] * s[i, q]
                    s[i, j] = s[i, j] - both * inverse
        blocks, belows = {}, {}
        for i in range(g + 1, min(g + 1 + near, panels)):
            block = ax_ref[ROWS * i : ROWS * (i + 1), :]
            below = []
            for k in range(ROWS):
                column = lane(block[:, :TILE], base + k)
                for m in range(k):
                    column = column - below[m] * low[k, m]
                below.append(column * r[k])
            blocks[i], belows[i] = block, below
        if g + 1 < panels:
            below = belows[g + 1]
            columns = [lane(blocks[g + 1][:, :TILE], base + ROWS + j) for j in range(ROWS)]
            for k in range(ROWS):
                below_ref[g % 2, k] = below[k]
                for j in range(ROWS):
                    columns[j] = columns[j] - below[k] * row(below_ref.at[g % 2, k], j, TILE)
        r2 = [jnp.concatenate([v, v], axis=1) for v in r]
        low2 = {key: jnp.concatenate([v, v], axis=1) for key, v in low.items()}
        z = []
        for k in range(ROWS):
            top = row(ax_ref, base + k, width)
            for m in range(k):
                top = top - low2[k, m] * z[m]
            z.append(top * r2[k])
        sub = lax.broadcasted_iota(jnp.int32, z[0].shape, 0)
        packed = z[0]
        for k in range(1, ROWS):
            packed = jnp.where(sub == k, z[k], packed)
        for i, block in blocks.items():
            for k in range(ROWS):
                block = block - jnp.concatenate([belows[i][k], belows[i][k]], axis=1) * z[k]
            ax_ref[ROWS * i : ROWS * (i + 1), :] = block
        ax_ref[base : base + ROWS, TILE:] = packed[:, TILE:]
        far = ROWS * (g + 1 + near)
        if far < ax_ref.shape[0]:
            a, b, c = three_parts(packed)
            left = jnp.concatenate([v[:, :TILE] for v in (a, a, b, b, a, c)], axis=0).astype(BF16)
            right = jnp.concatenate([a, b, a, b, c, a], axis=0).astype(BF16)
            product = bf_dot(left, right, TN)
            ax_ref[far:, :] = ax_ref[far:, :] - product[far:, :]
        between(g)


def add_product(j, live, acc_ref, source_ref, blocks_ref, rows_ref, cols_ref, row_base):
    to = pl.multiple_of((rows_ref[j] - row_base) * TILE, TILE)
    at = pl.multiple_of(cols_ref[j] * TILE, TILE)
    product = bf_dot(blocks_ref[j], source_ref[pl.ds(at, TILE), :], NN)
    if live is not None:
        product = jnp.where(live, product, 0.0)
    acc_ref[pl.ds(to, TILE), :] = acc_ref[pl.ds(to, TILE), :] + product


def add_pair(t, table_ref, acc_ref, source_ref, blocks_ref):
    a, b = table_ref[0, 2 * t], table_ref[0, 2 * t + 1]
    to = pl.multiple_of(table_ref[1, 2 * t] * TILE, TILE)
    at_a = pl.multiple_of(table_ref[2, 2 * t] * TILE, TILE)
    at_b = pl.multiple_of(table_ref[2, 2 * t + 1] * TILE, TILE)
    left = jnp.concatenate([blocks_ref[a], blocks_ref[b]], axis=1)
    right = jnp.concatenate(
        [source_ref[pl.ds(at_a, TILE), :], source_ref[pl.ds(at_b, TILE), :]], axis=0
    )
    acc_ref[pl.ds(to, TILE), :] = acc_ref[pl.ds(to, TILE), :] + bf_dot(left, right, NN)


def pair_table(rows, cols, count):
    shape = (TILE, TILE)
    i = lax.broadcasted_iota(jnp.int32, shape, 0)
    j = lax.broadcasted_iota(jnp.int32, shape, 1)
    row_j, col_j = (jnp.broadcast_to(v.astype(F32), shape) for v in (rows, cols))
    row_i, col_i = row_j.T, col_j.T
    ones, none = jnp.ones(shape, F32), jnp.zeros(shape, F32)
    same = (row_i == row_j) & (i < count)
    rank_j = jnp.sum(jnp.where(same & (i < j), ones, none), axis=0, keepdims=True)
    size_j = jnp.sum(jnp.where(same, ones, none), axis=0, keepdims=True)
    half = jnp.floor(size_j * 0.5)
    odd_last = (size_j - 2.0 * half) * jnp.where(rank_j == size_j - 1.0, 1.0, 0.0)
    ahead = jnp.where(row_j < row_i, ones + odd_last, none)
    ahead = ahead + jnp.where((row_j == row_i) & (j < i), ones, none)
    place_i = jnp.sum(jnp.where(j < count, ahead, none), axis=1, keepdims=True)
    match = (place_i == j.astype(F32)) & (i < count)
    found = jnp.sum(jnp.where(match, ones, none), axis=0, keepdims=True)
    block = jnp.sum(jnp.where(match, i.astype(F32), none), axis=0, keepdims=True)
    block = block + (1.0 - found) * count
    row_of = jnp.sum(jnp.where(match, row_i, none), axis=0, keepdims=True)
    col_of = jnp.sum(jnp.where(match, col_i, none), axis=0, keepdims=True)
    return jnp.concatenate([block, row_of, col_of], axis=0).astype(jnp.int32)


def factor_kernel(
    crows_ref,
    ccols_ref,
    rows_ref,
    cols_ref,
    next_hbm,
    u_hbm,
    blocks_hbm,
    cblocks_hbm,
    f_ref,
    packed_ref,
    yt_ref,
    w_ref,
    gram_ref,
    upper_ref,
    inv_ref,
    ax_ref,
    col_ref,
    below_ref,
    u_ref,
    turned_ref,
    blocks_ref,
    acc_ref,
    next_ref,
    cblocks_ref,
    hop_ref,
    m_ref,
    mt_ref,
    index_ref,
    made_ref,
    table_ref,
    sems,
    u_sems,
):
    orbitals, modes = u_ref.shape
    surface = hop_ref.shape[0]
    count = blocks_hbm.shape[0]
    slots = (count + orbitals // TILE) // 2
    tiles = modes // TILE
    panels = TILE // ROWS
    step = orbitals // panels
    chunks = u_sems.shape[0]
    long_step = orbitals // chunks
    copies = [
        pltpu.make_async_copy(
            u_hbm.at[pl.ds(c * long_step, long_step)],
            u_ref.at[pl.ds(c * long_step, long_step)],
            u_sems.at[c],
        )
        for c in range(chunks)
    ]
    more = [
        pltpu.make_async_copy(blocks_hbm, blocks_ref.at[pl.ds(0, count)], sems.at[0]),
        pltpu.make_async_copy(cblocks_hbm, cblocks_ref, sems.at[1]),
        pltpu.make_async_copy(next_hbm, next_ref, sems.at[2]),
    ]
    for copy in copies + more:
        copy.start()
    index_ref[...] = jnp.zeros_like(index_ref)
    index_ref[0:1, :count] = rows_ref[...]
    index_ref[1:2, :count] = cols_ref[...]
    made_ref[0:3, :] = pair_table(index_ref[0:1, :], index_ref[1:2, :], count)
    more.append(pltpu.make_async_copy(made_ref, table_ref, sems.at[3]))
    more[-1].start()
    blocks_ref[count] = jnp.zeros_like(blocks_ref[count])
    acc_ref[...] = jnp.zeros_like(acc_ref)
    hop_ref[...] = jnp.zeros_like(hop_ref)
    inv_ref[...] = jnp.zeros_like(inv_ref)

    def tile_of(t):
        return slice(t * TILE, (t + 1) * TILE)

    def gram_part(lo, hi, first, size):
        piece = slice(first, first + size)
        turned = u_ref[piece, lo:hi].T
        turned_ref[lo:hi, piece] = turned
        product = bf_dot(turned, u_ref[piece, lo:], NN)
        if first == 0:
            gram_ref[lo:hi, lo:] = product
        else:
            gram_ref[lo:hi, lo:] = gram_ref[lo:hi, lo:] + product

    for c, copy in enumerate(copies):
        copy.wait()
        gram_part(0, TILE, c * long_step, long_step)

    def wait_more():
        for copy in more:
            copy.wait()

    def onsite_product(t):
        add_pair(t, table_ref, acc_ref, u_ref, blocks_ref)

    def coupling_product(j):
        base = (orbitals - surface) // TILE
        add_product(j, None, hop_ref, next_ref, cblocks_ref, crows_ref, ccols_ref, base)

    def reduce_part(out_ref, base, source_ref, first):
        left = turned_ref[:, base + first : base + first + step]
        product = bf_dot(left, source_ref[first : first + step, :].astype(BF16), NN)
        out_ref[...] = product if first == 0 else out_ref[...] + product

    def schur(i, j, t):
        gram_ref[tile_of(i), tile_of(j)] = gram_ref[tile_of(i), tile_of(j)] - exact_dot(
            upper_ref[tile_of(t), tile_of(i)].T, upper_ref[tile_of(t), tile_of(j)]
        )

    def inverse_sum(i, t):
        width = slice(0, (t + 1) * TILE)
        inv_ref[tile_of(i), width] = inv_ref[tile_of(i), width] - exact_dot(
            upper_ref[tile_of(t), tile_of(i)].T, inv_ref[tile_of(t), width]
        )

    def inverse_row(i):
        width = slice(0, i * TILE)
        inv_ref[tile_of(i), width] = exact_dot(
            inv_ref[tile_of(i), tile_of(i)], inv_ref[tile_of(i), width]
        )

    call = functools.partial
    products = [call(onsite_product, t) for t in range(slots)]
    links = [call(coupling_product, j) for j in range(cblocks_ref.shape[0])]
    reductions = [call(reduce_part, w_ref, 0, acc_ref, c * step) for c in range(panels)]
    finish = [
        call(reduce_part, m_ref, orbitals - surface, hop_ref, first)
        for first in range(0, surface, step)
    ]
    plan = {(t, g): [] for t in range(tiles) for g in range(panels)}
    for g in range(panels):
        plan[0, g].append(call(gram_part, TILE, modes, g * step, step))
    plan[0, 3].append(wait_more)
    room = [(0, g) for g in range(4, panels)]
    room += [(t, g) for t in range(1, tiles - 1) for g in range(panels) for _ in range(2)]
    for n, work in enumerate(products):
        plan[room[n * len(room) // len(products)]].append(work)
    for n, work in enumerate(reductions):
        plan[tiles - 1, n * panels // len(reductions)].append(work)
    for n, work in enumerate(links):
        plan[tiles - 1, n * (panels // 2) // len(links)].append(work)
    for n, work in enumerate(finish):
        plan[tiles - 1, panels // 2 + n].append(work)
    ready = modes - TILE

    def turn_early():
        mt_ref[0], mt_ref[1] = split(m_ref[...].T)
        f_ref[:, :ready] = inv_ref[:ready, :].T.astype(BF16)

    def link_columns(columns):
        part = f_ref[:, columns]
        yt = bf_dot(mt_ref[0], part, NN) + bf_dot(mt_ref[1], part, NN)
        yt_ref[:, columns] = yt.astype(BF16)

    plan[tiles - 1, panels - 5].append(turn_early)
    plan[tiles - 1, panels - 3].append(call(link_columns, slice(0, ready)))
    for t in range(1, tiles):
        late = []
        if t > 1:
            late.append(call(inverse_row, t - 1))
        late += [call(schur, i, j, t - 1) for i in range(t, tiles) for j in range(i, tiles)][1:]
        late += [call(inverse_sum, i, t - 1) for i in range(t, tiles)]
        for n, work in enumerate(late):
            plan[t, n * (panels - 2) // len(late)].insert(0, work)

    def one_tile(t):
        here = tile_of(t)
        tile = gram_ref[here, here]
        on_diagonal = lax.broadcasted_iota(jnp.int32, tile.shape, 0) == lax.broadcasted_iota(
            jnp.int32, tile.shape, 1
        )
        diagonal = jnp.where(on_diagonal, tile, 0.0)
        across = lax.rsqrt(jnp.sum(diagonal, axis=0, keepdims=True))
        down = lax.rsqrt(jnp.sum(diagonal, axis=1, keepdims=True))
        ax_ref[:, :TILE] = tile * across * down
        ax_ref[:, TILE:] = on_diagonal.astype(F32)

        def between(g):
            for work in plan[t, g]:
                work()

        factor_tile(ax_ref, col_ref, below_ref, between)
        x = ax_ref[:, TILE:] * across
        inv_ref[here, here] = x
        if t + 1 < tiles:
            upper_ref[here, (t + 1) * TILE :] = exact_dot(x, gram_ref[here, (t + 1) * TILE :])
            schur(t + 1, t + 1, t)
        else:
            inverse_row(t)

    def step_of(b, carry):
        for t in range(tiles):
            pl.when(b == t)(call(one_tile, t))
        return carry

    lax.fori_loop(0, tiles, step_of, 0)
    last = inv_ref[ready:, :].T.astype(BF16)
    f_ref[:, ready:] = last
    link_columns(slice(ready, modes))
    packed_ref[:, :ready] = f_ref[:ready, :ready]
    packed_ref[:, ready:] = last[:ready, :]
    packed_ref[TILE:, :TILE] = last[ready:, :]


def couple_kernel(yt_ref, next_ref, f_ref, last_yt_ref, right_ref, left_ref, full_ref):
    full_ref[...] = jnp.zeros_like(full_ref)
    full_ref[:TILE, :] = next_ref[:TILE, :]
    full_ref[TILE : 2 * TILE, TILE:] = next_ref[TILE:, TILE:]
    full_ref[2 * TILE :, 2 * TILE :] = next_ref[TILE:, :TILE]
    right_ref[...] = bf_dot(yt_ref[...], full_ref[...], TN)
    left_ref[...] = bf_dot(f_ref[...], last_yt_ref[...], TN)


def split(value):
    high = value.astype(BF16)
    return high, (value - high.astype(F32)).astype(BF16)


def onsite_kernel(place_ref, w_ref, f_ref, steps_ref, out_ref):
    modes = f_ref.shape[0]
    w = w_ref[...]
    w = w + w.T
    f = f_ref[...]
    high, low = split(w)
    half = bf_dot(high, f, NN) + bf_dot(low, f, NN)
    high, low = split(half)
    full = bf_dot(f, high, TN) + bf_dot(f, low, TN)
    steps = steps_ref[...]
    reached = lax.broadcasted_iota(jnp.int32, steps.shape, 0) <= place_ref[0]
    potential = jnp.sum(jnp.where(reached, steps, 0.0), axis=0, keepdims=True)[:, :1]
    i = lax.broadcasted_iota(jnp.int32, (modes, modes), 0)
    j = lax.broadcasted_iota(jnp.int32, (modes, modes), 1)
    out_ref[...] = full + jnp.where(i == j, potential, 0.0)


def struct(shape, dtype):
    return jax.ShapeDtypeStruct(shape, dtype)


ANY = pl.BlockSpec(memory_space=pl.ANY)
INTO_VMEM = pl.BlockSpec(memory_space=pltpu.VMEM)
INTO_SMEM = pl.BlockSpec(memory_space=pltpu.SMEM)


def params(mebibytes):
    return pltpu.CompilerParams(vmem_limit_bytes=mebibytes * 1024 * 1024)


def passed_along(block, axis, distance):
    devices = range(lax.axis_size(axis))
    route = [(i - distance, i) for i in devices if i - distance in devices]
    return lax.ppermute(block, axis, route)


def cost(flops, moved):
    return pl.CostEstimate(flops=flops, bytes_accessed=moved, transcendentals=0)


def shards(
    trial_modes,
    onsite_blocks,
    onsite_rows,
    onsite_cols,
    coupling_blocks,
    coupling_rows,
    coupling_cols,
    potential_step,
):
    u = trial_modes[0]
    orbitals, modes = u.shape
    surface = SURFACE * TILE
    count = onsite_blocks.shape[1]
    links = coupling_blocks.shape[1]
    place = lax.axis_index("slab").astype(jnp.int32).reshape(1)
    slabs = lax.axis_size("slab")
    next_head = passed_along(u[:surface], "slab", -1)
    steps = lax.all_to_all(
        jnp.broadcast_to(potential_step[:, None], (slabs, TILE)), "slab", 0, 0, tiled=True
    )

    factor, packed, yt, w = pl.pallas_call(
        factor_kernel,
        out_shape=(
            struct((modes, modes), BF16),
            struct((modes - TILE, modes), BF16),
            struct((modes, modes), BF16),
            struct((modes, modes), F32),
        ),
        in_specs=[INTO_SMEM] * 2 + [INTO_VMEM] * 2 + [ANY] * 4,
        out_specs=(INTO_VMEM,) * 4,
        scratch_shapes=[
            pltpu.VMEM((modes, modes), F32),
            pltpu.VMEM((modes, modes), F32),
            pltpu.VMEM((modes, modes), F32),
            pltpu.VMEM((TILE, 2 * TILE), F32),
            pltpu.VMEM((2, ROWS, ROWS, TILE), F32),
            pltpu.VMEM((2, ROWS, ROWS, TILE), F32),
            pltpu.VMEM((orbitals, modes), BF16),
            pltpu.VMEM((modes, orbitals), BF16),
            pltpu.VMEM((count + 1, TILE, TILE), BF16),
            pltpu.VMEM((orbitals, modes), F32),
            pltpu.VMEM((surface, modes), BF16),
            pltpu.VMEM((links, TILE, TILE), BF16),
            pltpu.VMEM((surface, modes), F32),
            pltpu.VMEM((modes, modes), F32),
            pltpu.VMEM((2, modes, modes), BF16),
            pltpu.VMEM((ROWS, TILE), jnp.int32),
            pltpu.VMEM((ROWS, TILE), jnp.int32),
            pltpu.SMEM((ROWS, TILE), jnp.int32),
            pltpu.SemaphoreType.DMA((4,)),
            pltpu.SemaphoreType.DMA((8,)),
        ],
        compiler_params=params(59),
        cost_estimate=cost(8 * orbitals * modes * modes, orbitals * modes * 2),
        name="factor",
    )(
        coupling_rows[0],
        coupling_cols[0],
        onsite_rows,
        onsite_cols,
        next_head,
        u,
        onsite_blocks[0],
        coupling_blocks[0],
    )
    next_packed = passed_along(packed, "slab", -1)
    last_yt = passed_along(yt, "slab", 1)

    onsite = pl.pallas_call(
        onsite_kernel,
        out_shape=struct((modes, modes), F32),
        in_specs=[INTO_SMEM] + [INTO_VMEM] * 3,
        out_specs=INTO_VMEM,
        compiler_params=params(60),
        cost_estimate=cost(8 * orbitals * modes * modes, 4 * orbitals * modes),
        name="onsite",
    )(place, w, factor, steps)

    right, left = pl.pallas_call(
        couple_kernel,
        out_shape=(struct((modes, modes), F32),) * 2,
        in_specs=[INTO_VMEM] * 4,
        out_specs=(INTO_VMEM,) * 2,
        scratch_shapes=[pltpu.VMEM((modes, modes), BF16)],
        compiler_params=params(8),
        cost_estimate=cost(4 * modes * modes * modes, 8 * modes * modes),
        name="couple",
    )(yt, next_packed, factor, last_yt)
    return (onsite[None], right[None], left[None])


def solution(mesh):
    return jax.shard_map(
        shards,
        mesh=mesh,
        in_specs=(
            P(("groups", "slab"), None, None),
            P(("groups", "slab"), None, None, None),
            P(("groups", "slab"), None),
            P(("groups", "slab"), None),
            P(("groups", "slab"), None, None, None),
            P(("groups", "slab"), None),
            P(("groups", "slab"), None),
            P(("groups", "slab")),
        ),
        out_specs=(
            P(("groups", "slab"), None, None),
            P(("groups", "slab"), None, None),
            P(("groups", "slab"), None, None),
        ),
        check_vma=False,
    )
```
